32 devices in a mesh: segment: 4 (over z), dp: 8 (over y, x, core).
Axes of the slice: x: 2, y: 2, z: 4, core: 2. Of those that a mesh axis runs over, the one named last changes fastest.
Arguments:
- images: bfloat16 [32, 16, 16, 256], P('dp'), may hold values from -6 to 6
- latent: float32 [32, 512], P('dp'), may hold values from -6 to 6
- weight: bfloat16 [4, 3, 3, 256, 256], P('segment'), may hold values from -0.125 to 0.125
- affine: float32 [4, 512, 256], P('segment'), may hold values from -0.25 to 0.25
- biases: float32 [4, 256], P('segment'), may hold values from -0.5 to 0.5
- cotangent: bfloat16 [32, 16, 16, 256], P('dp'), may hold values from -6 to 6
Outputs:
- grad_weight: float32 [4, 3, 3, 256, 256], P('segment')
- grad_affine: float32 [4, 512, 256], P('segment')
- grad_bias: float32 [4, 256], P('segment')
- grad_latent: float32 [32, 512], P('dp')
The draws below stay inside these ranges and needn't reach their ends.
All inputs are finite; a program needn't handle non-finite values.
Results may differ from the reference program's by a relative error of at most 0.038.
Values may be sent and summed in bfloat16 or wider, within the bound.
A program may use at most 64 MiB of HBM per device.

```python
import math
import jax
import jax.numpy as jnp
from jax import lax

C = 256
WDIM = 512
RES = 16
MICRO = 1
LAYERS = 4
BATCH = 32


def levels(rng, dims, shards, low, largest):
    factor_of, own = 1.0, jax.random.fold_in(rng, 6)
    for dim, shards_of in shards:
        heights = jnp.exp(jax.random.uniform(jax.random.fold_in(own, dim), (shards_of,), jnp.float32, low / len(shards), largest / len(shards)))
        factor_of = factor_of * jnp.repeat(heights, dims[dim] // shards_of).reshape([-1 if axis == dim else 1 for axis in range(len(dims))])
    return factor_of


def normal_values(stream_key, dims, spread, reach, pieces=(), held_as=jnp.bfloat16):
    array = jax.random.normal(stream_key, dims, jnp.float32) * spread
    if len(pieces) > 0:
        array = levels(stream_key, dims, pieces, -0.22, 0.18) * array
    return jnp.clip(array, min=-reach, max=reach).astype(held_as)


def setup_inputs(seed: int = 0) -> dict:
    seeds = jax.random.split(jax.random.key(seed), 7)
    return {
        "images": normal_values(seeds[0], (BATCH, RES, RES, C), 1.0, 6.0, ((0, 8),)),
        "latent": normal_values(seeds[1], (BATCH, WDIM), 1.0, 6.0, ((0, 8),), jnp.float32),
        "weight": normal_values(seeds[2], (LAYERS, 3, 3, C, C), (9 * C) ** -0.5, 0.125, ((0, 4),)),
        "affine": normal_values(seeds[3], (LAYERS, WDIM, C), WDIM ** -0.5, 0.25, ((0, 4),), jnp.float32),
        "biases": jnp.clip(jax.random.uniform(seeds[4], (LAYERS, C), jnp.float32, -0.5, 0.5) * levels(seeds[4], (LAYERS, C), ((0, 4),), -0.4, 0.0), -0.5, 0.5),
        "cotangent": normal_values(seeds[5], (BATCH, RES, RES, C), 1.0, 6.0, ((0, 8),)),
    }


GAIN = math.sqrt(2.0)

def synth_layer(inputs, latent_rows, kernel, affine_map, offsets):
    styles = jnp.dot(latent_rows, affine_map, precision=lax.Precision.HIGHEST) + 1.0
    energy = lax.optimization_barrier(jnp.sum(jnp.square(kernel.astype(jnp.float32)), axis=(0, 1)))
    demodulate = lax.rsqrt(jnp.dot(styles * styles, energy, precision=lax.Precision.HIGHEST) + 1e-08)
    scaled = (inputs.astype(jnp.float32) * styles[:, None, None, :]).astype(jnp.bfloat16)
    convolved = lax.conv_general_dilated(scaled, kernel, (1, 1), 'SAME', dimension_numbers=('NHWC', 'HWIO', 'NHWC'), preferred_element_type=jnp.float32)
    hidden = convolved * demodulate[:, None, None, :] + offsets
    return (GAIN * hidden * (0.6 + 0.4 * jnp.tanh(hidden))).astype(jnp.bfloat16)

def reference(images, latent, weight, affine, biases, cotangent):
    group_count = BATCH // MICRO
    image_groups = images.reshape(group_count, MICRO, RES, RES, C)
    latent_groups = latent.reshape(group_count, MICRO, WDIM)
    upstream_groups = cotangent.reshape(group_count, MICRO, RES, RES, C)

    def one_group(totals, item):
        inputs, latent_rows, upstream = item
        stored = []
        current = inputs
        for level in range(LAYERS):
            stored.append(current)
            current = synth_layer(current, latent_rows, weight[level], affine[level], biases[level])
        weight_parts = [None] * LAYERS
        affine_parts = [None] * LAYERS
        bias_parts = [None] * LAYERS
        latent_total = jnp.zeros((MICRO, WDIM), jnp.float32)
        for level in reversed(range(LAYERS)):
            result, pull = jax.vjp(synth_layer, stored[level], latent_rows, weight[level], affine[level], biases[level])
            upstream, part_latent, part_weight, part_affine, part_bias = pull(upstream)
            weight_parts[level] = part_weight.astype(jnp.float32)
            affine_parts[level] = part_affine
            bias_parts[level] = part_bias
            latent_total = latent_total + part_latent
        grad_w, grad_a, grad_b = totals
        totals = (grad_w + jnp.stack(weight_parts), grad_a + jnp.stack(affine_parts), grad_b + jnp.stack(bias_parts))
        return (totals, latent_total)
    start = (jnp.zeros((LAYERS, 3, 3, C, C), jnp.float32), jnp.zeros((LAYERS, WDIM, C), jnp.float32), jnp.zeros((LAYERS, C), jnp.float32))
    totals, latent_out = lax.scan(one_group, start, (image_groups, latent_groups, upstream_groups))
    return (totals[0], totals[1], totals[2], latent_out.reshape(BATCH, WDIM))
```

```python
import functools
import math

import jax
import jax.numpy as jnp
from jax import lax
from jax.experimental import pallas as pl
from jax.experimental.pallas import tpu as pltpu
from jax.sharding import PartitionSpec as P

GAIN = math.sqrt(2.0)
MESH = pl.DeviceIdType.MESH
F32 = jnp.float32
BF16 = jnp.bfloat16
NN = (((1,), (0,)), ((), ()))
NT = (((1,), (1,)), ((), ()))
TN = (((0,), (0,)), ((), ()))


def exact(a, b, dims):
    return lax.dot_general(
        a, b, dims, precision=lax.Precision.HIGHEST, preferred_element_type=F32
    )


def relay(
    segments, width,
    images, latent, weight, affine, biases, cotangent,
    wgrad_out, rows_out, latent_out,
    fin, fout, gin, gout, spread_x, conv, slope, flipped, spread_g, acc, energy,
    styles, demod, d_demod, d_style, d_bias,
    f_send, f_recv, g_send, g_recv,
):
    count, pixels, chans = images.shape
    seg = lax.axis_index("segment")
    first, last = seg == 0, seg == segments - 1
    up, down = jnp.minimum(seg + 1, segments - 1), jnp.maximum(seg - 1, 0)

    barrier = pltpu.get_barrier_semaphore()

    @pl.when(jnp.logical_not(first))
    def _():
        pl.semaphore_signal(barrier, inc=1, device_id={"segment": down}, device_id_type=MESH)

    @pl.when(jnp.logical_not(last))
    def _():
        pl.semaphore_signal(barrier, inc=1, device_id={"segment": up}, device_id_type=MESH)

    pl.semaphore_wait(barrier, jnp.where(first, 0, 1) + jnp.where(last, 0, 1))

    def forward_copy(n):
        return pltpu.make_async_remote_copy(
            src_ref=fout.at[n], dst_ref=fin.at[n], send_sem=f_send.at[n],
            recv_sem=f_recv.at[n], device_id={"segment": up}, device_id_type=MESH,
        )

    def backward_copy(n):
        return pltpu.make_async_remote_copy(
            src_ref=gout.at[n], dst_ref=gin.at[n], send_sem=g_send.at[n],
            recv_sem=g_recv.at[n], device_id={"segment": down}, device_id_type=MESH,
        )

    column = lax.rem(lax.broadcasted_iota(jnp.int32, (pixels, chans), 0), width)
    at_left, at_right = column == 0, column == width - 1

    def spread(target, value):
        body = slice(width, width + pixels)
        target[body, chans:2 * chans] = value.astype(BF16)
        target[body, :chans] = jnp.where(at_left, 0.0, pltpu.roll(value, 1, 0)).astype(BF16)
        target[body, 2 * chans:] = jnp.where(
            at_right, 0.0, pltpu.roll(value, pixels - 1, 0)
        ).astype(BF16)

    def conv3(source, kernel):
        total = jnp.dot(source[0:pixels, :], kernel[0], preferred_element_type=F32)
        for dy in (1, 2):
            total += jnp.dot(
                source[dy * width:dy * width + pixels, :], kernel[dy], preferred_element_type=F32
            )
        return total

    total = jnp.zeros((chans, chans), F32)
    for dy in range(3):
        for dx in range(3):
            total += jnp.square(weight[dy, dx * chans:(dx + 1) * chans, :].astype(F32))
    energy[...] = total
    style_rows = exact(latent[...], affine[...], NN) + 1.0
    demod_rows = lax.rsqrt(exact(style_rows * style_rows, total, NN) + 1e-08)
    edge = jnp.zeros((width, 3 * chans), BF16)
    for n in range(count):
        styles[n] = style_rows[n:n + 1, :]
        demod[n] = demod_rows[n:n + 1, :]
        spread_x[n, 0:width, :] = edge
        spread_x[n, width + pixels:, :] = edge
    spread_g[0:width, :] = edge
    spread_g[width + pixels:, :] = edge

    def forward(n, carry):
        @pl.when(first)
        def _():
            fin[n] = images[n]

        @pl.when(jnp.logical_not(first))
        def _():
            forward_copy(n).wait_recv()

        spread(spread_x.at[n], fin[n].astype(F32) * styles[n])
        convolved = conv3(spread_x.at[n], weight)
        conv[n] = convolved
        hidden = convolved * demod[n] + biases[...]
        gate = jnp.tanh(hidden)
        fout[n] = (GAIN * hidden * (0.6 + 0.4 * gate)).astype(BF16)

        @pl.when(jnp.logical_not(last))
        def _():
            forward_copy(n).start()

        slope[n] = GAIN * (0.6 + 0.4 * gate + 0.4 * hidden * (1.0 - gate * gate))
        return carry

    lax.fori_loop(0, count, forward, 0)

    for dy in range(3):
        for dx in range(3):
            part = weight[2 - dy, (2 - dx) * chans:(3 - dx) * chans, :]
            flipped[dy, dx * chans:(dx + 1) * chans, :] = part.T
    acc[...] = jnp.zeros_like(acc)
    d_bias[...] = jnp.zeros_like(d_bias)

    def backward(n, carry):
        @pl.when(last)
        def _():
            gin[n] = cotangent[n]

        @pl.when(jnp.logical_not(last))
        def _():
            backward_copy(n).wait_recv()

        d_hidden = gin[n].astype(F32) * slope[n]
        d_conv = d_hidden * demod[n]
        spread(spread_g, d_conv)
        d_scaled = conv3(spread_g, flipped)
        gout[n] = (d_scaled * styles[n]).astype(BF16)

        @pl.when(jnp.logical_not(first))
        def _():
            backward_copy(n).start()

        d_style[n] = jnp.sum(d_scaled * fin[n].astype(F32), axis=0, keepdims=True)
        d_bias[...] += jnp.sum(d_hidden, axis=0, keepdims=True)
        d_demod[n] = jnp.sum(d_hidden * conv[n], axis=0, keepdims=True)
        turned = d_conv.astype(BF16).T
        for dy in range(3):
            acc[dy * chans:(dy + 1) * chans, :] += jnp.dot(
                turned, spread_x[n, dy * width:dy * width + pixels, :],
                preferred_element_type=F32,
            )
        return carry

    lax.fori_loop(0, count, backward, 0)

    wgrad_out[...] = acc[...].astype(BF16)
    style_rows = jnp.concatenate([styles[n] for n in range(count)], axis=0)
    demod_rows = jnp.concatenate([demod[n] for n in range(count)], axis=0)
    d_under = jnp.concatenate([d_demod[n] for n in range(count)], axis=0) * (
        -0.5 * demod_rows * demod_rows * demod_rows
    )
    d_rows = jnp.concatenate([d_style[n] for n in range(count)], axis=0)
    d_rows = d_rows + 2.0 * style_rows * exact(d_under, energy[...], NT)
    rows_out[0:count, :] = d_rows
    rows_out[count:2 * count, :] = d_under
    rows_out[2 * count:3 * count, :] = style_rows * style_rows
    rows_out[3 * count:3 * count + 1, :] = d_bias[...]
    latent_out[...] = exact(d_rows, affine[...], NT)

    def finish(n, carry):
        @pl.when(jnp.logical_not(last))
        def _():
            forward_copy(n).wait_send()

        @pl.when(jnp.logical_not(first))
        def _():
            backward_copy(n).wait_send()

        return carry

    lax.fori_loop(0, count, finish, 0)


def body(images, latent, weight, affine, biases, cotangent):
    count, height, width, chans = images.shape
    pixels = height * width
    kernel = weight[0]
    segments = lax.axis_size("segment")
    maps = (count, pixels, chans)
    row = (count, 1, chans)
    vmem = pl.BlockSpec(memory_space=pltpu.VMEM)
    dma = pltpu.SemaphoreType.DMA((count,))
    wgrad, rows, latent_part = pl.pallas_call(
        functools.partial(relay, segments, width),
        out_shape=(
            jax.ShapeDtypeStruct((3 * chans, 3 * chans), BF16),
            jax.ShapeDtypeStruct((3 * count + 1, chans), F32),
            jax.ShapeDtypeStruct(latent.shape, F32),
        ),
        in_specs=[vmem] * 6,
        out_specs=(vmem, vmem, vmem),
        scratch_shapes=[
            pltpu.VMEM(maps, BF16), pltpu.VMEM(maps, BF16),
            pltpu.VMEM(maps, BF16), pltpu.VMEM(maps, BF16),
            pltpu.VMEM((count, pixels + 2 * width, 3 * chans), BF16),
            pltpu.VMEM(maps, F32), pltpu.VMEM(maps, F32),
            pltpu.VMEM((3, 3 * chans, chans), BF16),
            pltpu.VMEM((pixels + 2 * width, 3 * chans), BF16),
            pltpu.VMEM((3 * chans, 3 * chans), F32),
            pltpu.VMEM((chans, chans), F32),
            pltpu.VMEM(row, F32), pltpu.VMEM(row, F32), pltpu.VMEM(row, F32),
            pltpu.VMEM(row, F32), pltpu.VMEM((1, chans), F32),
            dma, dma, dma, dma,
        ],
        compiler_params=pltpu.CompilerParams(
            collective_id=0, has_side_effects=True, vmem_limit_bytes=40 * 1024 * 1024
        ),
    )(
        images.reshape(maps), latent, kernel.reshape(3, 3 * chans, chans), affine[0], biases,
        cotangent.reshape(maps),
    )
    wgrad = lax.psum(wgrad, "dp").astype(F32)
    wgrad = wgrad.reshape(3, chans, 3, chans).transpose(0, 2, 3, 1)
    every = lax.all_gather(rows, "dp")
    latents = lax.all_gather(latent, "dp", tiled=True)
    d_rows = every[:, :count].reshape(-1, chans)
    d_under = every[:, count:2 * count].reshape(-1, chans)
    squares = every[:, 2 * count:3 * count].reshape(-1, chans)
    d_bias = jnp.sum(every[:, 3 * count], axis=0)
    wgrad = wgrad + 2.0 * kernel.astype(F32) * exact(squares, d_under, TN)
    d_affine = exact(latents, d_rows, TN)
    latent_total = lax.psum(latent_part, "segment")
    return (wgrad[None], d_affine[None], d_bias[None], latent_total)


def solution(mesh):
    placed = (
        P("dp", None, None, None),
        P("dp", None),
        P("segment", None, None, None, None),
        P("segment", None, None),
        P("segment", None),
        P("dp", None, None, None),
    )
    return jax.shard_map(
        body,
        mesh=mesh,
        in_specs=placed,
        out_specs=(
            P("segment", None, None, None, None),
            P("segment", None, None),
            P("segment", None),
            P("dp", None),
        ),
        check_vma=False,
    )
```

```python
import functools
import math

import jax
import jax.numpy as jnp
from jax import lax
from jax.experimental import pallas as pl
from jax.experimental.pallas import tpu as pltpu
from jax.sharding import PartitionSpec as P

GAIN = math.sqrt(2.0)
MESH = pl.DeviceIdType.MESH
F32 = jnp.float32
BF16 = jnp.bfloat16
NN = (((1,), (0,)), ((), ()))
NT = (((1,), (1,)), ((), ()))
TN = (((0,), (0,)), ((), ()))


def exact(a, b, dims):
    return lax.dot_general(
        a, b, dims, precision=lax.Precision.HIGHEST, preferred_element_type=F32
    )


def relay(
    segments, replicas, width,
    images, latent, weight_in, affine_in, biases_in, cotangent,
    wgrad, energy_grad, affine_grad, bias_grad, latent_grad,
    fin, fout, gin, gout, weight, affine, biases, latents,
    spread_x, turned_x, conv, slope, flipped, spread_g, acc, energy,
    styles, demod, d_demod, d_style, d_bias, rows, parts,
    pair_out, pair_in, chip_out, chip_in, own,
    f_send, f_recv, g_send, g_recv, loads, l_send, l_recv, r_send, r_recv, p_send, p_recv,
    a_send, a_recv, b_send, b_recv, c_send, c_recv, d_send, d_recv,
):
    count, pixels, chans = fin.shape
    chips = replicas // 2
    share = acc.shape[0] // replicas
    seg, me = lax.axis_index("segment"), lax.axis_index("dp")
    chip, core = me // 2, lax.rem(me, 2)
    partner = me + 1 - 2 * core
    first, last = seg == 0, seg == segments - 1
    up, down = jnp.minimum(seg + 1, segments - 1), jnp.maximum(seg - 1, 0)

    def remote(src, dst, send, recv, **device):
        return pltpu.make_async_remote_copy(
            src_ref=src, dst_ref=dst, send_sem=send, recv_sem=recv,
            device_id=device, device_id_type=MESH,
        )

    load_weight = pltpu.make_async_copy(weight_in, weight, loads.at[0])
    load_affine = pltpu.make_async_copy(affine_in, affine, loads.at[1])
    load_latent = pltpu.make_async_copy(latent, latents.at[me], loads.at[2])
    load_biases = pltpu.make_async_copy(biases_in, biases, loads.at[3])
    load_images = pltpu.make_async_copy(images, fin, loads.at[4])
    load_cotangent = pltpu.make_async_copy(cotangent, gin, loads.at[5])
    load_weight.start()
    load_affine.start()
    load_latent.start()
    load_biases.start()

    @pl.when(first)
    def _():
        load_images.start()

    @pl.when(last)
    def _():
        load_cotangent.start()

    barrier = pltpu.get_barrier_semaphore()
    for k in range(1, replicas):
        pl.semaphore_signal(
            barrier, inc=1, device_id={"dp": lax.rem(me + k, replicas)}, device_id_type=MESH
        )
    for k in range(1, segments):
        pl.semaphore_signal(
            barrier, inc=1, device_id={"segment": lax.rem(seg + k, segments)}, device_id_type=MESH
        )

    def forward_copy(n):
        return remote(fout.at[n], fin.at[n], f_send.at[n], f_recv.at[n], segment=up)

    def backward_copy(n):
        return remote(gout.at[n], gin.at[n], g_send.at[n], g_recv.at[n], segment=down)

    def latent_copy(k, owner):
        return remote(
            latents.at[owner], latents.at[owner], l_send.at[k], l_recv.at[k],
            dp=lax.rem(me + k, replicas),
        )

    def rows_copy(k, owner):
        return remote(
            rows.at[owner], rows.at[owner], r_send.at[k], r_recv.at[k],
            dp=lax.rem(me + k, replicas),
        )

    def parts_copy(k, owner):
        return remote(
            parts.at[owner], parts.at[owner], p_send.at[k], p_recv.at[k],
            segment=lax.rem(seg + k, segments),
        )

    column = lax.rem(lax.broadcasted_iota(jnp.int32, (pixels, chans), 0), width)
    at_left, at_right = column == 0, column == width - 1
    middle = slice(width, width + pixels)

    def spread(target, value):
        target[middle, chans:2 * chans] = value.astype(BF16)
        target[middle, :chans] = jnp.where(at_left, 0.0, pltpu.roll(value, 1, 0)).astype(BF16)
        target[middle, 2 * chans:] = jnp.where(
            at_right, 0.0, pltpu.roll(value, pixels - 1, 0)
        ).astype(BF16)

    def conv3(source, kernel):
        total = jnp.dot(source[0:pixels, :], kernel[0], preferred_element_type=F32)
        for dy in (1, 2):
            total += jnp.dot(
                source[dy * width:dy * width + pixels, :], kernel[dy], preferred_element_type=F32
            )
        return total

    edge = jnp.zeros((width, 3 * chans), BF16)
    for n in range(count):
        for target in (spread_x, spread_g):
            target[n, 0:width, :] = edge
            target[n, width + pixels:, :] = edge
    d_bias[...] = jnp.zeros_like(d_bias)
    load_weight.wait()
    total = jnp.zeros((chans, chans), F32)
    for dy in range(3):
        for dx in range(3):
            total += jnp.square(weight[dy, dx * chans:(dx + 1) * chans, :].astype(F32))
    energy[...] = total
    load_affine.wait()
    load_latent.wait()
    load_biases.wait()
    style_rows = exact(latents[me], affine[...], NN) + 1.0
    demod_rows = lax.rsqrt(exact(style_rows * style_rows, total, NN) + 1e-08)
    for n in range(count):
        styles[n] = style_rows[n:n + 1, :]
        demod[n] = demod_rows[n:n + 1, :]

    def flip():
        for dy in range(3):
            for dx in range(3):
                part = weight[2 - dy, (2 - dx) * chans:(3 - dx) * chans, :]
                flipped[dy, dx * chans:(dx + 1) * chans, :] = part.T

    @pl.when(first)
    def _():
        load_images.wait()

    @pl.when(last)
    def _():
        flip()
        load_cotangent.wait()

    pl.semaphore_wait(barrier, replicas + segments - 2)

    def forward(n):
        @pl.when(jnp.logical_not(first))
        def _():
            forward_copy(n).wait_recv()

        spread(spread_x.at[n], fin[n].astype(F32) * styles[n])
        convolved = conv3(spread_x.at[n], weight)
        conv[n] = convolved
        hidden = convolved * demod[n] + biases[...]
        gate = jnp.tanh(hidden)
        fout[n] = (GAIN * hidden * (0.6 + 0.4 * gate)).astype(BF16)

        @pl.when(jnp.logical_not(last))
        def _():
            forward_copy(n).start()

        slope[n] = GAIN * (0.6 + 0.4 * gate + 0.4 * hidden * (1.0 - gate * gate))

    def backward(n):
        d_hidden = gin[n].astype(F32) * slope[n]
        spread(spread_g.at[n], d_hidden * demod[n])
        d_scaled = conv3(spread_g.at[n], flipped)
        gout[n] = (d_scaled * styles[n]).astype(BF16)

        @pl.when(jnp.logical_not(first))
        def _():
            backward_copy(n).start()

        d_style[n] = jnp.sum(d_scaled * fin[n].astype(F32), axis=0, keepdims=True)
        d_bias[...] += jnp.sum(d_hidden, axis=0, keepdims=True)
        d_demod[n] = jnp.sum(d_hidden * conv[n], axis=0, keepdims=True)

    def forward_step(n, carry):
        forward(n)

        @pl.when(last)
        def _():
            backward(n)

        turned_x[n] = spread_x[n, middle, chans:2 * chans].T
        return carry

    lax.fori_loop(0, count, forward_step, 0)

    @pl.when(jnp.logical_not(last))
    def _():
        flip()

    for k in range(1, replicas):
        latent_copy(k, me).start()
    acc[...] = jnp.zeros_like(acc)

    def backward_step(n, carry):
        @pl.when(jnp.logical_not(last))
        def _():
            backward_copy(n).wait_recv()
            backward(n)

        for dy in range(3):
            block = jnp.dot(
                turned_x[n], spread_g[n, dy * width:dy * width + pixels, :],
                preferred_element_type=F32,
            )
            for dx in range(3):
                start = ((2 - dy) * 3 + 2 - dx) * chans
                acc[start:start + chans, :] += block[:, dx * chans:(dx + 1) * chans]
        return carry

    lax.fori_loop(0, count, backward_step, 0)

    def acc_share(half, q):
        start = pl.multiple_of((half * chips + q) * share, share)
        return acc[pl.ds(start, share), :]

    def pair_copy(k):
        return remote(pair_out.at[k], pair_in.at[k], a_send.at[k], a_recv.at[k], dp=partner)

    def chip_copy(k):
        return remote(
            chip_out.at[k], chip_in.at[k], b_send.at[k], b_recv.at[k],
            dp=2 * lax.rem(chip + k, chips) + core,
        )

    def shard_copy(k, q):
        return remote(
            wgrad.at[core, q], wgrad.at[core, q], c_send.at[k], c_recv.at[k],
            dp=2 * lax.rem(chip + k, chips) + core,
        )

    def relay_copy(k, half, q):
        return remote(
            wgrad.at[half, q], wgrad.at[half, q], d_send.at[k], d_recv.at[k], dp=partner
        )

    order = list(range(1, chips)) + [0]
    for k in order:
        pair_out[k] = acc_share(1 - core, lax.rem(chip + k, chips)).astype(BF16)
        pair_copy(k).start()
    for k in order:
        pair_copy(k).wait_recv()
        both = acc_share(core, lax.rem(chip + k, chips)) + pair_in[k].astype(F32)
        if k:
            chip_out[k] = both.astype(BF16)
            chip_copy(k).start()
        else:
            own[...] = both

    style_rows = jnp.concatenate([styles[n] for n in range(count)], axis=0)
    demod_rows = jnp.concatenate([demod[n] for n in range(count)], axis=0)
    d_under = jnp.concatenate([d_demod[n] for n in range(count)], axis=0) * (
        -0.5 * demod_rows * demod_rows * demod_rows
    )
    d_rows = jnp.concatenate([d_style[n] for n in range(count)], axis=0)
    d_rows = d_rows + 2.0 * style_rows * exact(d_under, energy[...], NT)
    rows[me, 0] = d_rows
    rows[me, 1] = d_under
    rows[me, 2] = style_rows * style_rows
    rows[me, 3] = jnp.broadcast_to(d_bias[...], (count, chans))
    for k in range(1, replicas):
        rows_copy(k, me).start()
    parts[seg] = exact(d_rows, affine[...], NT)
    for k in range(1, segments):
        parts_copy(k, seg).start()

    reduced = own[...]
    for k in range(1, chips):
        chip_copy(k).wait_recv()
        reduced += chip_in[k].astype(F32)
    wgrad[core, chip] = reduced.astype(BF16)
    for k in range(1, chips):
        shard_copy(k, chip).start()
    relay_copy(0, core, chip).start()

    for k in range(1, replicas):
        owner = lax.rem(me + replicas - k, replicas)
        latent_copy(k, owner).wait_recv()
        rows_copy(k, owner).wait_recv()
    d_rows = jnp.concatenate([rows[d, 0] for d in range(replicas)], axis=0)
    d_under = jnp.concatenate([rows[d, 1] for d in range(replicas)], axis=0)
    squares = jnp.concatenate([rows[d, 2] for d in range(replicas)], axis=0)
    every = jnp.concatenate([latents[d] for d in range(replicas)], axis=0)
    energy_grad[...] = 2.0 * exact(squares, d_under, TN)
    affine_grad[...] = exact(every, d_rows, TN)
    bias_total = rows[0, 3]
    for d in range(1, replicas):
        bias_total += rows[d, 3]
    bias_grad[...] = bias_total[0:1, :]

    for k in range(1, chips):
        q = lax.rem(chip + chips - k, chips)
        shard_copy(k, q).wait_recv()
        relay_copy(k, core, q).start()

    for k in range(1, segments):
        parts_copy(k, lax.rem(seg + segments - k, segments)).wait_recv()
    latent_total = parts[0]
    for s in range(1, segments):
        latent_total += parts[s]
    latent_grad[...] = latent_total

    for k in range(chips):
        relay_copy(k, 1 - core, lax.rem(chip + chips - k, chips)).wait_recv()

    def finish(n, carry):
        @pl.when(jnp.logical_not(last))
        def _():
            forward_copy(n).wait_send()

        @pl.when(jnp.logical_not(first))
        def _():
            backward_copy(n).wait_send()

        return carry

    lax.fori_loop(0, count, finish, 0)
    for k in range(1, replicas):
        latent_copy(k, me).wait_send()
        rows_copy(k, me).wait_send()
    for k in range(1, segments):
        parts_copy(k, seg).wait_send()
    for k in range(chips):
        pair_copy(k).wait_send()
        relay_copy(k, core, lax.rem(chip + chips - k, chips)).wait_send()
        if k:
            chip_copy(k).wait_send()
            shard_copy(k, chip).wait_send()


def body(images, latent, weight, affine, biases, cotangent):
    count, height, width, chans = images.shape
    pixels = height * width
    kernel = weight[0]
    segments, replicas = lax.axis_size("segment"), lax.axis_size("dp")
    chips = replicas // 2
    taps = 9 * chans
    share = taps // replicas
    maps = (count, pixels, chans)
    row = (count, 1, chans)
    tall = (count, pixels + 2 * width, 3 * chans)
    vmem = pl.BlockSpec(memory_space=pltpu.VMEM)
    here = pl.BlockSpec(memory_space=pl.ANY)
    dma = pltpu.SemaphoreType.DMA
    wgrad, energy_grad, affine_grad, bias_grad, latent_grad = pl.pallas_call(
        functools.partial(relay, segments, replicas, width),
        out_shape=(
            jax.ShapeDtypeStruct((2, chips, share, chans), BF16),
            jax.ShapeDtypeStruct((chans, chans), F32),
            jax.ShapeDtypeStruct(affine.shape[1:], F32),
            jax.ShapeDtypeStruct((1, chans), F32),
            jax.ShapeDtypeStruct(latent.shape, F32),
        ),
        in_specs=[here] * 6,
        out_specs=(vmem,) * 5,
        scratch_shapes=[
            pltpu.VMEM(maps, BF16), pltpu.VMEM(maps, BF16),
            pltpu.VMEM(maps, BF16), pltpu.VMEM(maps, BF16),
            pltpu.VMEM((3, 3 * chans, chans), BF16),
            pltpu.VMEM(affine.shape[1:], F32),
            pltpu.VMEM((1, chans), F32),
            pltpu.VMEM((replicas,) + latent.shape, F32),
            pltpu.VMEM(tall, BF16),
            pltpu.VMEM((count, chans, pixels), BF16),
            pltpu.VMEM(maps, F32), pltpu.VMEM(maps, F32),
            pltpu.VMEM((3, 3 * chans, chans), BF16),
            pltpu.VMEM(tall, BF16),
            pltpu.VMEM((taps, chans), F32),
            pltpu.VMEM((chans, chans), F32),
            pltpu.VMEM(row, F32), pltpu.VMEM(row, F32), pltpu.VMEM(row, F32),
            pltpu.VMEM(row, F32), pltpu.VMEM((1, chans), F32),
            pltpu.VMEM((replicas, 4, count, chans), F32),
            pltpu.VMEM((segments,) + latent.shape, F32),
            pltpu.VMEM((chips, share, chans), BF16), pltpu.VMEM((chips, share, chans), BF16),
            pltpu.VMEM((chips, share, chans), BF16), pltpu.VMEM((chips, share, chans), BF16),
            pltpu.VMEM((share, chans), F32),
            dma((count,)), dma((count,)), dma((count,)), dma((count,)), dma((6,)),
            dma((replicas,)), dma((replicas,)), dma((replicas,)), dma((replicas,)),
            dma((segments,)), dma((segments,)),
            dma((chips,)), dma((chips,)), dma((chips,)), dma((chips,)),
            dma((chips,)), dma((chips,)), dma((chips,)), dma((chips,)),
        ],
        compiler_params=pltpu.CompilerParams(
            collective_id=0, has_side_effects=True, vmem_limit_bytes=56 * 1024 * 1024
        ),
    )(
        images.reshape(maps), latent, kernel.reshape(3, 3 * chans, chans), affine[0], biases,
        cotangent.reshape(maps),
    )
    wgrad = wgrad.reshape(kernel.shape).astype(F32) + kernel.astype(F32) * energy_grad
    return (wgrad[None], affine_grad[None], bias_grad, latent_grad)


def solution(mesh):
    placed = (
        P("dp", None, None, None),
        P("dp", None),
        P("segment", None, None, None, None),
        P("segment", None, None),
        P("segment", None),
        P("dp", None, None, None),
    )
    return jax.shard_map(
        body,
        mesh=mesh,
        in_specs=placed,
        out_specs=(
            P("segment", None, None, None, None),
            P("segment", None, None),
            P("segment", None),
            P("dp", None),
        ),
        check_vma=False,
    )
```

```python
import functools
import math

import jax
import jax.numpy as jnp
from jax import lax
from jax.experimental import pallas as pl
from jax.experimental.pallas import tpu as pltpu
from jax.sharding import PartitionSpec as P

GAIN = math.sqrt(2.0)
MESH = pl.DeviceIdType.MESH
F32 = jnp.float32
BF16 = jnp.bfloat16
NN = (((1,), (0,)), ((), ()))
NT = (((1,), (1,)), ((), ()))
TN = (((0,), (0,)), ((), ()))


def exact(a, b, dims):
    return lax.dot_general(
        a, b, dims, precision=lax.Precision.HIGHEST, preferred_element_type=F32
    )


def relay(
    segments, replicas, width,
    images, latent, weight_in, affine_in, biases_in, cotangent,
    wgrad, energy_grad, affine_grad, bias_grad, latent_grad,
    fin, fout, gin, gout, weight, affine, biases, latents,
    spread_x, turned_x, conv, slope, flipped, spread_g, acc, energy,
    styles, demod, d_demod, d_style, d_bias, rows, parts,
    pair_out, pair_in, chip_out, chip_in, own,
    f_send, f_recv, g_send, g_recv, loads, l_send, l_recv, r_send, r_recv, p_send, p_recv,
    a_send, a_recv, b_send, b_recv, c_send, c_recv, d_send, d_recv,
):
    count, pixels, chans = fin.shape
    chips = replicas // 2
    share = acc.shape[0] // replicas
    seg, me = lax.axis_index("segment"), lax.axis_index("dp")
    chip, core = me // 2, lax.rem(me, 2)
    partner = me + 1 - 2 * core
    first, last = seg == 0, seg == segments - 1

    def remote(src, dst, send, recv, **device):
        return pltpu.make_async_remote_copy(
            src_ref=src, dst_ref=dst, send_sem=send, recv_sem=recv,
            device_id=device, device_id_type=MESH,
        )

    load_weight = pltpu.make_async_copy(weight_in, weight, loads.at[0])
    load_affine = pltpu.make_async_copy(affine_in, affine, loads.at[1])
    load_latent = pltpu.make_async_copy(latent, latents.at[me], loads.at[2])
    load_biases = pltpu.make_async_copy(biases_in, biases, loads.at[3])
    load_images = pltpu.make_async_copy(images, fin, loads.at[4])
    load_cotangent = pltpu.make_async_copy(cotangent, gin, loads.at[5])
    load_weight.start()
    load_affine.start()
    load_latent.start()
    load_biases.start()

    @pl.when(first)
    def _():
        load_images.start()

    @pl.when(last)
    def _():
        load_cotangent.start()

    barrier = pltpu.get_barrier_semaphore()
    for k in range(1, replicas):
        pl.semaphore_signal(
            barrier, inc=1, device_id={"dp": lax.rem(me + k, replicas)}, device_id_type=MESH
        )
    for k in range(1, segments):
        pl.semaphore_signal(
            barrier, inc=1, device_id={"segment": lax.rem(seg + k, segments)}, device_id_type=MESH
        )

    def rows_of(cut, piece):
        return (0, cut * width) if piece == 0 else (cut * width, pixels - cut * width)

    def cut_at(hops):
        return pixels // width // 2 + segments // 2 - 1 - hops

    def forward_copy(n, piece, cut, to):
        block = pl.ds(*rows_of(cut, piece))
        return remote(
            fout.at[n, block], fin.at[n, block], f_send.at[n, piece], f_recv.at[n, piece],
            segment=to,
        )

    def backward_copy(n, piece, cut, to):
        block = pl.ds(*rows_of(cut, piece))
        return remote(
            gout.at[n, block], gin.at[n, block], g_send.at[n, piece], g_recv.at[n, piece],
            segment=to,
        )

    def latent_copy(k, owner):
        return remote(
            latents.at[owner], latents.at[owner], l_send.at[k], l_recv.at[k],
            dp=lax.rem(me + k, replicas),
        )

    def rows_copy(k, owner):
        return remote(
            rows.at[owner], rows.at[owner], r_send.at[k], r_recv.at[k],
            dp=lax.rem(me + k, replicas),
        )

    def parts_copy(k, owner):
        return remote(
            parts.at[owner], parts.at[owner], p_send.at[k], p_recv.at[k],
            segment=lax.rem(seg + k, segments),
        )

    middle = slice(width, width + pixels)

    def spread(target, value, start):
        size = value.shape[0]
        column = lax.rem(lax.broadcasted_iota(jnp.int32, (size, chans), 0), width)
        block = slice(width + start, width + start + size)
        target[block, chans:2 * chans] = value.astype(BF16)
        target[block, :chans] = jnp.where(
            column == 0, 0.0, pltpu.roll(value, 1, 0)
        ).astype(BF16)
        target[block, 2 * chans:] = jnp.where(
            column == width - 1, 0.0, pltpu.roll(value, size - 1, 0)
        ).astype(BF16)

    def conv3(source, kernel, start, size):
        total = jnp.dot(source[start:start + size, :], kernel[0], preferred_element_type=F32)
        for dy in (1, 2):
            at = start + dy * width
            total += jnp.dot(source[at:at + size, :], kernel[dy], preferred_element_type=F32)
        return total

    edge = jnp.zeros((width, 3 * chans), BF16)
    for n in range(count):
        for target in (spread_x, spread_g):
            target[n, 0:width, :] = edge
            target[n, width + pixels:, :] = edge
    d_bias[...] = jnp.zeros_like(d_bias)
    load_weight.wait()
    total = jnp.zeros((chans, chans), F32)
    for dy in range(3):
        for dx in range(3):
            total += jnp.square(weight[dy, dx * chans:(dx + 1) * chans, :].astype(F32))
    energy[...] = total
    load_affine.wait()
    load_latent.wait()
    load_biases.wait()
    style_rows = exact(latents[me], affine[...], NN) + 1.0
    demod_rows = lax.rsqrt(exact(style_rows * style_rows, total, NN) + 1e-08)
    for n in range(count):
        styles[n] = style_rows[n:n + 1, :]
        demod[n] = demod_rows[n:n + 1, :]

    def flip():
        for dy in range(3):
            for dx in range(3):
                part = weight[2 - dy, (2 - dx) * chans:(3 - dx) * chans, :]
                flipped[dy, dx * chans:(dx + 1) * chans, :] = part.T

    pl.semaphore_wait(barrier, replicas + segments - 2)

    def forward(n, index):
        cut = cut_at(index)
        for piece in range(2):
            start, size = rows_of(cut + 1, piece)
            if index > 0:
                forward_copy(n, piece, cut + 1, index - 1).wait_recv()
            spread(
                spread_x.at[n], fin[n, start:start + size, :].astype(F32) * styles[n], start
            )
            start, size = rows_of(cut, piece)
            block = slice(start, start + size)
            convolved = conv3(spread_x.at[n], weight, start, size)
            hidden = convolved * demod[n] + biases[...]
            gate = jnp.tanh(hidden)
            if index < segments - 1:
                fout[n, block, :] = (GAIN * hidden * (0.6 + 0.4 * gate)).astype(BF16)
                forward_copy(n, piece, cut, index + 1).start()
            conv[n, block, :] = convolved
            slope[n, block, :] = GAIN * (0.6 + 0.4 * gate + 0.4 * hidden * (1.0 - gate * gate))

    def backward(n, index):
        cut = cut_at(segments - 1 - index)
        for piece in range(2):
            start, size = rows_of(cut + 1, piece)
            block = slice(start, start + size)
            if index < segments - 1:
                backward_copy(n, piece, cut + 1, index + 1).wait_recv()
            d_hidden = gin[n, block, :].astype(F32) * slope[n, block, :]
            spread(spread_g.at[n], d_hidden * demod[n], start)
            start, size = rows_of(cut, piece)
            out = slice(start, start + size)
            d_scaled = conv3(spread_g.at[n], flipped, start, size)
            if index > 0:
                gout[n, out, :] = (d_scaled * styles[n]).astype(BF16)
                backward_copy(n, piece, cut, index - 1).start()
            style_part = jnp.sum(d_scaled * fin[n, out, :].astype(F32), axis=0, keepdims=True)
            demod_part = jnp.sum(d_hidden * conv[n, block, :], axis=0, keepdims=True)
            d_style[n] = style_part if piece == 0 else d_style[n] + style_part
            d_demod[n] = demod_part if piece == 0 else d_demod[n] + demod_part
            d_bias[...] += jnp.sum(d_hidden, axis=0, keepdims=True)

    def add_weight_grad(n):
        for dy in range(3):
            block = jnp.dot(
                turned_x[n], spread_g[n, dy * width:dy * width + pixels, :],
                preferred_element_type=F32,
            )
            for dx in range(3):
                start = ((2 - dy) * 3 + 2 - dx) * chans
                acc[start:start + chans, :] += block[:, dx * chans:(dx + 1) * chans]

    def section(index):
        if index == 0:
            load_images.wait()
        if index == segments - 1:
            flip()
            load_cotangent.wait()

        def forward_step(n, carry):
            forward(n, index)
            if index == segments - 1:
                backward(n, index)
            turned_x[n] = spread_x[n, middle, chans:2 * chans].T
            return carry

        lax.fori_loop(0, count, forward_step, 0)
        if index < segments - 1:
            flip()
        for k in range(1, replicas):
            latent_copy(k, me).start()
        acc[...] = jnp.zeros_like(acc)

        def backward_step(n, carry):
            if index < segments - 1:
                backward(n, index)
            add_weight_grad(n)
            return carry

        lax.fori_loop(0, count, backward_step, 0)

        def finish(n, carry):
            for piece in range(2):
                if index < segments - 1:
                    forward_copy(n, piece, cut_at(index), index + 1).wait_send()
                if index > 0:
                    backward_copy(
                        n, piece, cut_at(segments - 1 - index), index - 1
                    ).wait_send()
            return carry

        lax.fori_loop(0, count, finish, 0)

    for index in range(segments):
        pl.when(seg == index)(functools.partial(section, index))

    def acc_share(half, q):
        start = pl.multiple_of((half * chips + q) * share, share)
        return acc[pl.ds(start, share), :]

    def pair_copy(k):
        return remote(pair_out.at[k], pair_in.at[k], a_send.at[k], a_recv.at[k], dp=partner)

    def chip_copy(k):
        return remote(
            chip_out.at[k], chip_in.at[k], b_send.at[k], b_recv.at[k],
            dp=2 * lax.rem(chip + k, chips) + core,
        )

    def shard_copy(k, q):
        return remote(
            wgrad.at[core, q], wgrad.at[core, q], c_send.at[k], c_recv.at[k],
            dp=2 * lax.rem(chip + k, chips) + core,
        )

    def relay_copy(k, half, q):
        return remote(
            wgrad.at[half, q], wgrad.at[half, q], d_send.at[k], d_recv.at[k], dp=partner
        )

    order = list(range(1, chips)) + [0]
    for k in order:
        pair_out[k] = acc_share(1 - core, lax.rem(chip + k, chips)).astype(BF16)
        pair_copy(k).start()
    for k in order:
        pair_copy(k).wait_recv()
        both = acc_share(core, lax.rem(chip + k, chips)) + pair_in[k].astype(F32)
        if k:
            chip_out[k] = both.astype(BF16)
            chip_copy(k).start()
        else:
            own[...] = both

    style_rows = jnp.concatenate([styles[n] for n in range(count)], axis=0)
    demod_rows = jnp.concatenate([demod[n] for n in range(count)], axis=0)
    d_under = jnp.concatenate([d_demod[n] for n in range(count)], axis=0) * (
        -0.5 * demod_rows * demod_rows * demod_rows
    )
    d_rows = jnp.concatenate([d_style[n] for n in range(count)], axis=0)
    d_rows = d_rows + 2.0 * style_rows * exact(d_under, energy[...], NT)
    rows[me, 0] = d_rows
    rows[me, 1] = d_under
    rows[me, 2] = style_rows * style_rows
    rows[me, 3] = jnp.broadcast_to(d_bias[...], (count, chans))
    for k in range(1, replicas):
        rows_copy(k, me).start()
    parts[seg] = exact(d_rows, affine[...], NT)
    for k in range(1, segments):
        parts_copy(k, seg).start()

    reduced = own[...]
    for k in range(1, chips):
        chip_copy(k).wait_recv()
        reduced += chip_in[k].astype(F32)
    wgrad[core, chip] = reduced.astype(BF16)
    for k in range(1, chips):
        shard_copy(k, chip).start()
    relay_copy(0, core, chip).start()

    for k in range(1, replicas):
        owner = lax.rem(me + replicas - k, replicas)
        latent_copy(k, owner).wait_recv()
        rows_copy(k, owner).wait_recv()
    d_rows = jnp.concatenate([rows[d, 0] for d in range(replicas)], axis=0)
    d_under = jnp.concatenate([rows[d, 1] for d in range(replicas)], axis=0)
    squares = jnp.concatenate([rows[d, 2] for d in range(replicas)], axis=0)
    every = jnp.concatenate([latents[d] for d in range(replicas)], axis=0)
    energy_grad[...] = 2.0 * exact(squares, d_under, TN)
    affine_grad[...] = exact(every, d_rows, TN)
    bias_total = rows[0, 3]
    for d in range(1, replicas):
        bias_total += rows[d, 3]
    bias_grad[...] = bias_total[0:1, :]

    for k in range(1, chips):
        q = lax.rem(chip + chips - k, chips)
        shard_copy(k, q).wait_recv()
        relay_copy(k, core, q).start()

    for k in range(1, segments):
        parts_copy(k, lax.rem(seg + segments - k, segments)).wait_recv()
    latent_total = parts[0]
    for s in range(1, segments):
        latent_total += parts[s]
    latent_grad[...] = latent_total

    for k in range(chips):
        relay_copy(k, 1 - core, lax.rem(chip + chips - k, chips)).wait_recv()

    for k in range(1, replicas):
        latent_copy(k, me).wait_send()
        rows_copy(k, me).wait_send()
    for k in range(1, segments):
        parts_copy(k, seg).wait_send()
    for k in range(chips):
        pair_copy(k).wait_send()
        relay_copy(k, core, lax.rem(chip + chips - k, chips)).wait_send()
        if k:
            chip_copy(k).wait_send()
            shard_copy(k, chip).wait_send()


def results(
    wgrad, weight, energy_grad, affine_in, bias_in, latent_in, weight_out, affine_out, bias_out,
    latent_out,
):
    chans = weight.shape[1]
    for start in range(0, weight.shape[0], chans):
        block = slice(start, start + chans)
        weight_out[block, :] = (
            wgrad[block, :].astype(F32) + weight[block, :].astype(F32) * energy_grad[...]
        )

    @pl.when(pl.program_id(0) == 0)
    def _():
        affine_out[...] = affine_in[...]
        bias_out[...] = bias_in[...]
        latent_out[...] = latent_in[...]


def body(images, latent, weight, affine, biases, cotangent):
    count, height, width, chans = images.shape
    pixels = height * width
    kernel = weight[0]
    segments, replicas = lax.axis_size("segment"), lax.axis_size("dp")
    chips = replicas // 2
    taps = 9 * chans
    share = taps // replicas
    maps = (count, pixels, chans)
    row = (count, 1, chans)
    tall = (count, pixels + 2 * width, 3 * chans)
    vmem = pl.BlockSpec(memory_space=pltpu.VMEM)
    here = pl.BlockSpec(memory_space=pl.ANY)
    dma = pltpu.SemaphoreType.DMA
    wgrad, energy_grad, affine_grad, bias_grad, latent_grad = pl.pallas_call(
        functools.partial(relay, segments, replicas, width),
        out_shape=(
            jax.ShapeDtypeStruct((2, chips, share, chans), BF16),
            jax.ShapeDtypeStruct((chans, chans), F32),
            jax.ShapeDtypeStruct(affine.shape[1:], F32),
            jax.ShapeDtypeStruct((1, chans), F32),
            jax.ShapeDtypeStruct(latent.shape, F32),
        ),
        in_specs=[here] * 6,
        out_specs=(vmem,) * 5,
        scratch_shapes=[
            pltpu.VMEM(maps, BF16), pltpu.VMEM(maps, BF16),
            pltpu.VMEM(maps, BF16), pltpu.VMEM(maps, BF16),
            pltpu.VMEM((3, 3 * chans, chans), BF16),
            pltpu.VMEM(affine.shape[1:], F32),
            pltpu.VMEM((1, chans), F32),
            pltpu.VMEM((replicas,) + latent.shape, F32),
            pltpu.VMEM(tall, BF16),
            pltpu.VMEM((count, chans, pixels), BF16),
            pltpu.VMEM(maps, F32), pltpu.VMEM(maps, F32),
            pltpu.VMEM((3, 3 * chans, chans), BF16),
            pltpu.VMEM(tall, BF16),
            pltpu.VMEM((taps, chans), F32),
            pltpu.VMEM((chans, chans), F32),
            pltpu.VMEM(row, F32), pltpu.VMEM(row, F32), pltpu.VMEM(row, F32),
            pltpu.VMEM(row, F32), pltpu.VMEM((1, chans), F32),
            pltpu.VMEM((replicas, 4, count, chans), F32),
            pltpu.VMEM((segments,) + latent.shape, F32),
            pltpu.VMEM((chips, share, chans), BF16), pltpu.VMEM((chips, share, chans), BF16),
            pltpu.VMEM((chips, share, chans), BF16), pltpu.VMEM((chips, share, chans), BF16),
            pltpu.VMEM((share, chans), F32),
            dma((count, 2)), dma((count, 2)), dma((count, 2)), dma((count, 2)), dma((6,)),
            dma((replicas,)), dma((replicas,)), dma((replicas,)), dma((replicas,)),
            dma((segments,)), dma((segments,)),
            dma((chips,)), dma((chips,)), dma((chips,)), dma((chips,)),
            dma((chips,)), dma((chips,)), dma((chips,)), dma((chips,)),
        ],
        compiler_params=pltpu.CompilerParams(
            collective_id=0, has_side_effects=True, vmem_limit_bytes=56 * 1024 * 1024
        ),
    )(
        images.reshape(maps), latent, kernel.reshape(3, 3 * chans, chans), affine[0], biases,
        cotangent.reshape(maps),
    )
    def whole(array):
        return pl.BlockSpec(array.shape, lambda step: (0, 0))

    block = pl.BlockSpec((3 * chans, chans), lambda step: (step, 0))
    small = (affine_grad, bias_grad, latent_grad)
    weight_grad, affine_grad, bias_grad, latent_grad = pl.pallas_call(
        results,
        grid=(3,),
        out_shape=(
            jax.ShapeDtypeStruct((taps, chans), F32),
            *[jax.ShapeDtypeStruct(array.shape, F32) for array in small],
        ),
        in_specs=[block, block, whole(energy_grad), *map(whole, small)],
        out_specs=(block, *map(whole, small)),
        compiler_params=pltpu.CompilerParams(vmem_limit_bytes=56 * 1024 * 1024),
    )(wgrad.reshape(taps, chans), kernel.reshape(taps, chans), energy_grad, *small)
    return (weight_grad.reshape(weight.shape), affine_grad[None], bias_grad, latent_grad)


def solution(mesh):
    placed = (
        P("dp", None, None, None),
        P("dp", None),
        P("segment", None, None, None, None),
        P("segment", None, None),
        P("segment", None),
        P("dp", None, None, None),
    )
    return jax.shard_map(
        body,
        mesh=mesh,
        in_specs=placed,
        out_specs=(
            P("segment", None, None, None, None),
            P("segment", None, None),
            P("segment", None),
            P("dp", None),
        ),
        check_vma=False,
    )
```

```python
import functools
import math

import jax
import jax.numpy as jnp
from jax import lax
from jax.experimental import pallas as pl
from jax.experimental.pallas import tpu as pltpu
from jax.sharding import PartitionSpec as P

GAIN = math.sqrt(2.0)
MESH = pl.DeviceIdType.MESH
F32 = jnp.float32
BF16 = jnp.bfloat16
NN = (((1,), (0,)), ((), ()))
NT = (((1,), (1,)), ((), ()))
TN = (((0,), (0,)), ((), ()))


def exact(a, b, dims):
    return lax.dot_general(
        a, b, dims, precision=lax.Precision.HIGHEST, preferred_element_type=F32
    )


def relay(
    segments, replicas, width,
    images, latent, weight_in, affine_in, biases_in, cotangent,
    wgrad, energy_grad, affine_grad, bias_grad, latent_grad,
    fin, fout, gin, gout, weight, affine, biases, latents,
    spread_x, turned_x, conv, slope, d_scaled, flipped, spread_g, acc, energy,
    styles, demod, d_demod, d_style, d_bias, rows, parts,
    pair_out, pair_in, chip_out, chip_in, own,
    f_send, f_recv, g_send, g_recv, loads, l_send, l_recv, r_send, r_recv, p_send, p_recv,
    a_send, a_recv, b_send, b_recv, c_send, c_recv, d_send, d_recv,
):
    count, pixels, chans = fin.shape
    chips = replicas // 2
    share = acc.shape[0] // replicas
    seg, me = lax.axis_index("segment"), lax.axis_index("dp")
    chip, core = me // 2, lax.rem(me, 2)
    partner = me + 1 - 2 * core
    first, last = seg == 0, seg == segments - 1

    def remote(src, dst, send, recv, **device):
        return pltpu.make_async_remote_copy(
            src_ref=src, dst_ref=dst, send_sem=send, recv_sem=recv,
            device_id=device, device_id_type=MESH,
        )

    load_weight = pltpu.make_async_copy(weight_in, weight, loads.at[0])
    load_affine = pltpu.make_async_copy(affine_in, affine, loads.at[1])
    load_latent = pltpu.make_async_copy(latent, latents.at[me], loads.at[2])
    load_biases = pltpu.make_async_copy(biases_in, biases, loads.at[3])
    load_images = pltpu.make_async_copy(images, fin, loads.at[4])
    load_cotangent = pltpu.make_async_copy(cotangent, gin, loads.at[5])
    load_weight.start()
    load_affine.start()
    load_latent.start()
    load_biases.start()

    @pl.when(first)
    def _():
        load_images.start()

    @pl.when(last)
    def _():
        load_cotangent.start()

    barrier = pltpu.get_barrier_semaphore()
    for k in range(1, replicas):
        pl.semaphore_signal(
            barrier, inc=1, device_id={"dp": lax.rem(me + k, replicas)}, device_id_type=MESH
        )
    for k in range(1, segments):
        pl.semaphore_signal(
            barrier, inc=1, device_id={"segment": lax.rem(seg + k, segments)}, device_id_type=MESH
        )

    def rows_of(cut, piece):
        return (0, cut * width) if piece == 0 else (cut * width, pixels - cut * width)

    def cut_at(hops):
        return pixels // width // 2 + segments // 2 - 1 - hops

    def forward_copy(n, piece, cut, to):
        block = pl.ds(*rows_of(cut, piece))
        return remote(
            fout.at[n, block], fin.at[n, block], f_send.at[n, piece], f_recv.at[n, piece],
            segment=to,
        )

    def backward_copy(n, piece, cut, to):
        block = pl.ds(*rows_of(cut, piece))
        return remote(
            gout.at[n, block], gin.at[n, block], g_send.at[n, piece], g_recv.at[n, piece],
            segment=to,
        )

    def latent_copy(k, owner):
        return remote(
            latents.at[owner], latents.at[owner], l_send.at[k], l_recv.at[k],
            dp=lax.rem(me + k, replicas),
        )

    def rows_copy(k, owner):
        return remote(
            rows.at[owner], rows.at[owner], r_send.at[k], r_recv.at[k],
            dp=lax.rem(me + k, replicas),
        )

    def parts_copy(k, owner):
        return remote(
            parts.at[owner], parts.at[owner], p_send.at[k], p_recv.at[k],
            segment=lax.rem(seg + k, segments),
        )

    middle = slice(width, width + pixels)

    def spread(target, value, start):
        size = value.shape[0]
        column = lax.rem(lax.broadcasted_iota(jnp.int32, (size, chans), 0), width)
        block = slice(width + start, width + start + size)
        target[block, chans:2 * chans] = value.astype(BF16)
        target[block, :chans] = jnp.where(
            column == 0, 0.0, pltpu.roll(value, 1, 0)
        ).astype(BF16)
        target[block, 2 * chans:] = jnp.where(
            column == width - 1, 0.0, pltpu.roll(value, size - 1, 0)
        ).astype(BF16)

    def conv3(source, kernel, start, size):
        total = jnp.dot(source[start:start + size, :], kernel[0], preferred_element_type=F32)
        for dy in (1, 2):
            at = start + dy * width
            total += jnp.dot(source[at:at + size, :], kernel[dy], preferred_element_type=F32)
        return total

    edge = jnp.zeros((width, 3 * chans), BF16)
    for n in range(count):
        for target in (spread_x, spread_g):
            target[n, 0:width, :] = edge
            target[n, width + pixels:, :] = edge
    d_bias[...] = jnp.zeros_like(d_bias)
    load_weight.wait()
    total = jnp.zeros((chans, chans), F32)
    for dy in range(3):
        for dx in range(3):
            total += jnp.square(weight[dy, dx * chans:(dx + 1) * chans, :].astype(F32))
    energy[...] = total
    load_affine.wait()
    load_latent.wait()
    load_biases.wait()
    style_rows = exact(latents[me], affine[...], NN) + 1.0
    demod_rows = lax.rsqrt(exact(style_rows * style_rows, total, NN) + 1e-08)
    for n in range(count):
        styles[n] = style_rows[n:n + 1, :]
        demod[n] = demod_rows[n:n + 1, :]

    def flip():
        for dy in range(3):
            for dx in range(3):
                part = weight[2 - dy, (2 - dx) * chans:(3 - dx) * chans, :]
                flipped[dy, dx * chans:(dx + 1) * chans, :] = part.T

    pl.semaphore_wait(barrier, replicas + segments - 2)

    def forward(n, index):
        cut = cut_at(index)
        for piece in range(2):
            start, size = rows_of(cut + 1, piece)
            if index > 0:
                forward_copy(n, piece, cut + 1, index - 1).wait_recv()
            spread(
                spread_x.at[n], fin[n, start:start + size, :].astype(F32) * styles[n], start
            )
            start, size = rows_of(cut, piece)
            block = slice(start, start + size)
            convolved = conv3(spread_x.at[n], weight, start, size)
            hidden = convolved * demod[n] + biases[...]
            gate = jnp.tanh(hidden)
            if index < segments - 1:
                fout[n, block, :] = (GAIN * hidden * (0.6 + 0.4 * gate)).astype(BF16)
                forward_copy(n, piece, cut, index + 1).start()
            conv[n, block, :] = convolved
            slope[n, block, :] = GAIN * (0.6 + 0.4 * gate + 0.4 * hidden * (1.0 - gate * gate))

    def arrive(n, index, piece):
        cut = cut_at(segments - 1 - index)
        start, size = rows_of(cut + 1, piece)
        block = slice(start, start + size)
        if index < segments - 1:
            backward_copy(n, piece, cut + 1, index + 1).wait_recv()
        spread(
            spread_g.at[n], gin[n, block, :].astype(F32) * (slope[n, block, :] * demod[n]), start
        )

    def push_back(n, index, piece):
        cut = cut_at(segments - 1 - index)
        start, size = rows_of(cut, piece)
        out = slice(start, start + size)
        back = conv3(spread_g.at[n], flipped, start, size)
        if index > 0:
            gout[n, out, :] = (back * styles[n]).astype(BF16)
            backward_copy(n, piece, cut, index - 1).start()
        d_scaled[n, out, :] = back

    def backward(n, index):
        for piece in range(2):
            arrive(n, index, piece)
            push_back(n, index, piece)

    def channel_sums(n):
        d_hidden = gin[n].astype(F32) * slope[n]
        d_bias[...] += jnp.sum(d_hidden, axis=0, keepdims=True)
        d_demod[n] = jnp.sum(d_hidden * conv[n], axis=0, keepdims=True)
        d_style[n] = jnp.sum(d_scaled[n] * fin[n].astype(F32), axis=0, keepdims=True)

    def add_weight_grad(n):
        for dy in range(3):
            block = jnp.dot(
                turned_x[n], spread_g[n, dy * width:dy * width + pixels, :],
                preferred_element_type=F32,
            )
            for dx in range(3):
                start = ((2 - dy) * 3 + 2 - dx) * chans
                acc[start:start + chans, :] += block[:, dx * chans:(dx + 1) * chans]

    def section(index):
        if index == 0:
            load_images.wait()
        if index == segments - 1:
            flip()
            load_cotangent.wait()

        def forward_step(n, carry):
            forward(n, index)
            if index == segments - 1:
                backward(n, index)
            return carry

        lax.fori_loop(0, count, forward_step, 0)
        if index < segments - 1:
            flip()
        for k in range(1, replicas):
            latent_copy(k, me).start()
        acc[...] = jnp.zeros_like(acc)

        def turn(n, carry):
            turned_x[n] = spread_x[n, middle, chans:2 * chans].T
            return carry

        lax.fori_loop(0, count, turn, 0)

        def backward_step(n, carry):
            if index < segments - 1:
                backward(n, index)
            channel_sums(n)
            add_weight_grad(n)
            return carry

        lax.fori_loop(0, count - 1 if index == 0 else count, backward_step, 0)
        if index == 0:
            for piece in range(2):
                arrive(count - 1, index, piece)
            add_weight_grad(count - 1)

        def finish(n, carry):
            for piece in range(2):
                if index < segments - 1:
                    forward_copy(n, piece, cut_at(index), index + 1).wait_send()
                if index > 0:
                    backward_copy(
                        n, piece, cut_at(segments - 1 - index), index - 1
                    ).wait_send()
            return carry

        lax.fori_loop(0, count, finish, 0)

    for index in range(segments):
        pl.when(seg == index)(functools.partial(section, index))

    def acc_share(half, q):
        start = pl.multiple_of((half * chips + q) * share, share)
        return acc[pl.ds(start, share), :]

    def pair_copy(k):
        return remote(pair_out.at[k], pair_in.at[k], a_send.at[k], a_recv.at[k], dp=partner)

    def chip_copy(k):
        return remote(
            chip_out.at[k], chip_in.at[k], b_send.at[k], b_recv.at[k],
            dp=2 * lax.rem(chip + k, chips) + core,
        )

    def shard_copy(k, q):
        return remote(
            wgrad.at[core, q], wgrad.at[core, q], c_send.at[k], c_recv.at[k],
            dp=2 * lax.rem(chip + k, chips) + core,
        )

    def relay_copy(k, half, q):
        return remote(
            wgrad.at[half, q], wgrad.at[half, q], d_send.at[k], d_recv.at[k], dp=partner
        )

    order = list(range(1, chips)) + [0]
    for k in order:
        pair_out[k] = acc_share(1 - core, lax.rem(chip + k, chips)).astype(BF16)
        pair_copy(k).start()

    @pl.when(first)
    def _():
        for piece in range(2):
            push_back(count - 1, 0, piece)
        channel_sums(count - 1)

    for k in order:
        pair_copy(k).wait_recv()
        both = acc_share(core, lax.rem(chip + k, chips)) + pair_in[k].astype(F32)
        if k:
            chip_out[k] = both.astype(BF16)
            chip_copy(k).start()
        else:
            own[...] = both

    style_rows = jnp.concatenate([styles[n] for n in range(count)], axis=0)
    demod_rows = jnp.concatenate([demod[n] for n in range(count)], axis=0)
    d_under = jnp.concatenate([d_demod[n] for n in range(count)], axis=0) * (
        -0.5 * demod_rows * demod_rows * demod_rows
    )
    d_rows = jnp.concatenate([d_style[n] for n in range(count)], axis=0)
    d_rows = d_rows + 2.0 * style_rows * exact(d_under, energy[...], NT)
    rows[me, 0] = d_rows
    rows[me, 1] = d_under
    rows[me, 2] = style_rows * style_rows
    rows[me, 3] = jnp.broadcast_to(d_bias[...], (count, chans))
    for k in range(1, replicas):
        rows_copy(k, me).start()
    parts[seg] = exact(d_rows, affine[...], NT)
    for k in range(1, segments):
        parts_copy(k, seg).start()

    reduced = own[...]
    for k in range(1, chips):
        chip_copy(k).wait_recv()
        reduced += chip_in[k].astype(F32)
    wgrad[core, chip] = reduced.astype(BF16)
    for k in range(1, chips):
        shard_copy(k, chip).start()
    relay_copy(0, core, chip).start()

    for k in range(1, replicas):
        owner = lax.rem(me + replicas - k, replicas)
        latent_copy(k, owner).wait_recv()
        rows_copy(k, owner).wait_recv()
    d_rows = jnp.concatenate([rows[d, 0] for d in range(replicas)], axis=0)
    d_under = jnp.concatenate([rows[d, 1] for d in range(replicas)], axis=0)
    squares = jnp.concatenate([rows[d, 2] for d in range(replicas)], axis=0)
    every = jnp.concatenate([latents[d] for d in range(replicas)], axis=0)
    energy_grad[...] = 2.0 * exact(squares, d_under, TN)
    affine_grad[...] = exact(every, d_rows, TN)
    bias_total = rows[0, 3]
    for d in range(1, replicas):
        bias_total += rows[d, 3]
    bias_grad[...] = bias_total[0:1, :]

    for k in range(1, chips):
        q = lax.rem(chip + chips - k, chips)
        shard_copy(k, q).wait_recv()
        relay_copy(k, core, q).start()

    for k in range(1, segments):
        parts_copy(k, lax.rem(seg + segments - k, segments)).wait_recv()
    latent_total = parts[0]
    for s in range(1, segments):
        latent_total += parts[s]
    latent_grad[...] = latent_total

    for k in range(chips):
        relay_copy(k, 1 - core, lax.rem(chip + chips - k, chips)).wait_recv()

    for k in range(1, replicas):
        latent_copy(k, me).wait_send()
        rows_copy(k, me).wait_send()
    for k in range(1, segments):
        parts_copy(k, seg).wait_send()
    for k in range(chips):
        pair_copy(k).wait_send()
        relay_copy(k, core, lax.rem(chip + chips - k, chips)).wait_send()
        if k:
            chip_copy(k).wait_send()
            shard_copy(k, chip).wait_send()


def results(
    wgrad, weight, energy_grad, affine_in, bias_in, latent_in, weight_out, affine_out, bias_out,
    latent_out, wgrad_here, weight_here, energy_here, out_here, in_sems, out_sems, small_sems,
):
    chans = weight.shape[1]
    blocks = [pl.ds(start, chans) for start in range(0, weight.shape[0], chans)]
    loads, stores = [], []
    load_energy = pltpu.make_async_copy(energy_grad, energy_here, small_sems.at[0])
    load_energy.start()
    for tap, block in enumerate(blocks):
        pair = (
            pltpu.make_async_copy(wgrad.at[block], wgrad_here.at[block], in_sems.at[0, tap]),
            pltpu.make_async_copy(weight.at[block], weight_here.at[block], in_sems.at[1, tap]),
        )
        for copy in pair:
            copy.start()
        loads.append(pair)
    small = [
        pltpu.make_async_copy(source, target, small_sems.at[place])
        for place, (source, target) in enumerate(
            ((affine_in, affine_out), (bias_in, bias_out), (latent_in, latent_out)), 1
        )
    ]
    for copy in small:
        copy.start()
    load_energy.wait()
    for tap, block in enumerate(blocks):
        for copy in loads[tap]:
            copy.wait()
        out_here[block, :] = (
            wgrad_here[block, :].astype(F32)
            + weight_here[block, :].astype(F32) * energy_here[...]
        )
        store = pltpu.make_async_copy(out_here.at[block], weight_out.at[block], out_sems.at[tap])
        store.start()
        stores.append(store)
    for copy in stores + small:
        copy.wait()


def body(images, latent, weight, affine, biases, cotangent):
    count, height, width, chans = images.shape
    pixels = height * width
    kernel = weight[0]
    segments, replicas = lax.axis_size("segment"), lax.axis_size("dp")
    chips = replicas // 2
    taps = 9 * chans
    share = taps // replicas
    maps = (count, pixels, chans)
    row = (count, 1, chans)
    tall = (count, pixels + 2 * width, 3 * chans)
    vmem = pl.BlockSpec(memory_space=pltpu.VMEM)
    here = pl.BlockSpec(memory_space=pl.ANY)
    dma = pltpu.SemaphoreType.DMA
    wgrad, energy_grad, affine_grad, bias_grad, latent_grad = pl.pallas_call(
        functools.partial(relay, segments, replicas, width),
        out_shape=(
            jax.ShapeDtypeStruct((2, chips, share, chans), BF16),
            jax.ShapeDtypeStruct((chans, chans), F32),
            jax.ShapeDtypeStruct(affine.shape[1:], F32),
            jax.ShapeDtypeStruct((1, chans), F32),
            jax.ShapeDtypeStruct(latent.shape, F32),
        ),
        in_specs=[here] * 6,
        out_specs=(vmem,) * 5,
        scratch_shapes=[
            pltpu.VMEM(maps, BF16), pltpu.VMEM(maps, BF16),
            pltpu.VMEM(maps, BF16), pltpu.VMEM(maps, BF16),
            pltpu.VMEM((3, 3 * chans, chans), BF16),
            pltpu.VMEM(affine.shape[1:], F32),
            pltpu.VMEM((1, chans), F32),
            pltpu.VMEM((replicas,) + latent.shape, F32),
            pltpu.VMEM(tall, BF16),
            pltpu.VMEM((count, chans, pixels), BF16),
            pltpu.VMEM(maps, F32), pltpu.VMEM(maps, F32), pltpu.VMEM(maps, F32),
            pltpu.VMEM((3, 3 * chans, chans), BF16),
            pltpu.VMEM(tall, BF16),
            pltpu.VMEM((taps, chans), F32),
            pltpu.VMEM((chans, chans), F32),
            pltpu.VMEM(row, F32), pltpu.VMEM(row, F32), pltpu.VMEM(row, F32),
            pltpu.VMEM(row, F32), pltpu.VMEM((1, chans), F32),
            pltpu.VMEM((replicas, 4, count, chans), F32),
            pltpu.VMEM((segments,) + latent.shape, F32),
            pltpu.VMEM((chips, share, chans), BF16), pltpu.VMEM((chips, share, chans), BF16),
            pltpu.VMEM((chips, share, chans), BF16), pltpu.VMEM((chips, share, chans), BF16),
            pltpu.VMEM((share, chans), F32),
            dma((count, 2)), dma((count, 2)), dma((count, 2)), dma((count, 2)), dma((6,)),
            dma((replicas,)), dma((replicas,)), dma((replicas,)), dma((replicas,)),
            dma((segments,)), dma((segments,)),
            dma((chips,)), dma((chips,)), dma((chips,)), dma((chips,)),
            dma((chips,)), dma((chips,)), dma((chips,)), dma((chips,)),
        ],
        compiler_params=pltpu.CompilerParams(
            collective_id=0, has_side_effects=True, vmem_limit_bytes=56 * 1024 * 1024
        ),
    )(
        images.reshape(maps), latent, kernel.reshape(3, 3 * chans, chans), affine[0], biases,
        cotangent.reshape(maps),
    )
    small = (affine_grad, bias_grad, latent_grad)
    weight_grad, affine_grad, bias_grad, latent_grad = pl.pallas_call(
        results,
        out_shape=(
            jax.ShapeDtypeStruct((taps, chans), F32),
            *[jax.ShapeDtypeStruct(array.shape, F32) for array in small],
        ),
        in_specs=[here] * 6,
        out_specs=(here,) * 4,
        scratch_shapes=[
            pltpu.VMEM((taps, chans), BF16), pltpu.VMEM((taps, chans), BF16),
            pltpu.VMEM((chans, chans), F32), pltpu.VMEM((taps, chans), F32),
            dma((2, 9)), dma((9,)), dma((4,)),
        ],
        compiler_params=pltpu.CompilerParams(vmem_limit_bytes=56 * 1024 * 1024),
    )(wgrad.reshape(taps, chans), kernel.reshape(taps, chans), energy_grad, *small)
    return (weight_grad.reshape(weight.shape), affine_grad[None], bias_grad, latent_grad)


def solution(mesh):
    placed = (
        P("dp", None, None, None),
        P("dp", None),
        P("segment", None, None, None, None),
        P("segment", None, None),
        P("segment", None),
        P("dp", None, None, None),
    )
    return jax.shard_map(
        body,
        mesh=mesh,
        in_specs=placed,
        out_specs=(
            P("segment", None, None, None, None),
            P("segment", None, None),
            P("segment", None),
            P("dp", None),
        ),
        check_vma=False,
    )
```

```python
import functools
import math

import jax
import jax.numpy as jnp
from jax import lax
from jax.experimental import pallas as pl
from jax.experimental.pallas import tpu as pltpu
from jax.sharding import PartitionSpec as P

GAIN = math.sqrt(2.0)
MESH = pl.DeviceIdType.MESH
F32 = jnp.float32
BF16 = jnp.bfloat16
NN = (((1,), (0,)), ((), ()))
NT = (((1,), (1,)), ((), ()))
TN = (((0,), (0,)), ((), ()))


def exact(a, b, dims):
    return lax.dot_general(
        a, b, dims, precision=lax.Precision.HIGHEST, preferred_element_type=F32
    )


def relay(
    segments, replicas, width,
    images, latent, weight_in, affine_in, biases_in, cotangent,
    wgrad, energy_grad, affine_grad, bias_grad, latent_grad,
    fin, fout, gin, gout, weight, affine, biases, latents,
    spread_x, turned_x, conv, slope, d_scaled, flipped, spread_g, acc, energy,
    styles, demod, d_demod, d_style, d_bias, rows, parts,
    pair_out, pair_in, chip_out, chip_in, own,
    f_send, f_recv, g_send, g_recv, loads, l_send, l_recv, r_send, r_recv, p_send, p_recv,
    a_send, a_recv, b_send, b_recv, c_send, c_recv, d_send, d_recv,
):
    count, pixels, chans = fin.shape
    chips = replicas // 2
    share = acc.shape[0] // replicas
    seg, me = lax.axis_index("segment"), lax.axis_index("dp")
    chip, core = me // 2, lax.rem(me, 2)
    partner = me + 1 - 2 * core
    first, last = seg == 0, seg == segments - 1

    def remote(src, dst, send, recv, **device):
        return pltpu.make_async_remote_copy(
            src_ref=src, dst_ref=dst, send_sem=send, recv_sem=recv,
            device_id=device, device_id_type=MESH,
        )

    load_weight = pltpu.make_async_copy(weight_in, weight, loads.at[0])
    load_affine = pltpu.make_async_copy(affine_in, affine, loads.at[1])
    load_latent = pltpu.make_async_copy(latent, latents.at[me], loads.at[2])
    load_biases = pltpu.make_async_copy(biases_in, biases, loads.at[3])
    load_images = pltpu.make_async_copy(images, fin, loads.at[4])
    load_cotangent = pltpu.make_async_copy(cotangent, gin, loads.at[5])
    load_weight.start()
    load_affine.start()
    load_latent.start()
    load_biases.start()

    @pl.when(first)
    def _():
        load_images.start()

    @pl.when(last)
    def _():
        load_cotangent.start()

    barrier = pltpu.get_barrier_semaphore()
    for k in range(1, replicas):
        pl.semaphore_signal(
            barrier, inc=1, device_id={"dp": lax.rem(me + k, replicas)}, device_id_type=MESH
        )
    for k in range(1, segments):
        pl.semaphore_signal(
            barrier, inc=1, device_id={"segment": lax.rem(seg + k, segments)}, device_id_type=MESH
        )

    def rows_of(cut, piece):
        return (0, cut * width) if piece == 0 else (cut * width, pixels - cut * width)

    def cut_at(hops):
        return pixels // width // 2 + segments // 2 - 1 - hops

    def forward_copy(n, piece, cut, to):
        block = pl.ds(*rows_of(cut, piece))
        return remote(
            fout.at[n, block], fin.at[n, block], f_send.at[n, piece], f_recv.at[n, piece],
            segment=to,
        )

    def backward_copy(n, piece, cut, to):
        block = pl.ds(*rows_of(cut, piece))
        return remote(
            gout.at[n, block], gin.at[n, block], g_send.at[n, piece], g_recv.at[n, piece],
            segment=to,
        )

    def latent_copy(k, owner):
        return remote(
            latents.at[owner], latents.at[owner], l_send.at[k], l_recv.at[k],
            dp=lax.rem(me + k, replicas),
        )

    def rows_copy(k, owner):
        return remote(
            rows.at[owner], rows.at[owner], r_send.at[k], r_recv.at[k],
            dp=lax.rem(me + k, replicas),
        )

    def parts_copy(k, owner):
        return remote(
            parts.at[owner], parts.at[owner], p_send.at[k], p_recv.at[k],
            segment=lax.rem(seg + k, segments),
        )

    middle = slice(width, width + pixels)

    def spread(target, value, start):
        size = value.shape[0]
        column = lax.rem(lax.broadcasted_iota(jnp.int32, (size, chans), 0), width)
        block = slice(width + start, width + start + size)
        target[block, chans:2 * chans] = value.astype(BF16)
        target[block, :chans] = jnp.where(
            column == 0, 0.0, pltpu.roll(value, 1, 0)
        ).astype(BF16)
        target[block, 2 * chans:] = jnp.where(
            column == width - 1, 0.0, pltpu.roll(value, size - 1, 0)
        ).astype(BF16)

    def conv3(source, kernel, start, size):
        total = jnp.dot(source[start:start + size, :], kernel[0], preferred_element_type=F32)
        for dy in (1, 2):
            at = start + dy * width
            total += jnp.dot(source[at:at + size, :], kernel[dy], preferred_element_type=F32)
        return total

    edge = jnp.zeros((width, 3 * chans), BF16)
    for n in range(count):
        for target in (spread_x, spread_g):
            target[n, 0:width, :] = edge
            target[n, width + pixels:, :] = edge
    d_bias[...] = jnp.zeros_like(d_bias)
    load_weight.wait()
    total = jnp.zeros((chans, chans), F32)
    for dy in range(3):
        for dx in range(3):
            total += jnp.square(weight[dy, dx * chans:(dx + 1) * chans, :].astype(F32))
    energy[...] = total
    load_affine.wait()
    load_latent.wait()
    load_biases.wait()
    style_rows = exact(latents[me], affine[...], NN) + 1.0
    demod_rows = lax.rsqrt(exact(style_rows * style_rows, total, NN) + 1e-08)
    for n in range(count):
        styles[n] = style_rows[n:n + 1, :]
        demod[n] = demod_rows[n:n + 1, :]

    def flip():
        for dy in range(3):
            for dx in range(3):
                part = weight[2 - dy, (2 - dx) * chans:(3 - dx) * chans, :]
                flipped[dy, dx * chans:(dx + 1) * chans, :] = part.T

    pl.semaphore_wait(barrier, replicas + segments - 2)

    def forward(n, index):
        cut = cut_at(index)
        for piece in range(2):
            start, size = rows_of(cut + 1, piece)
            if index > 0:
                forward_copy(n, piece, cut + 1, index - 1).wait_recv()
            spread(
                spread_x.at[n], fin[n, start:start + size, :].astype(F32) * styles[n], start
            )
            start, size = rows_of(cut, piece)
            block = slice(start, start + size)
            convolved = conv3(spread_x.at[n], weight, start, size)
            hidden = convolved * demod[n] + biases[...]
            gate = jnp.tanh(hidden)
            if index < segments - 1:
                fout[n, block, :] = (GAIN * hidden * (0.6 + 0.4 * gate)).astype(BF16)
                forward_copy(n, piece, cut, index + 1).start()
            conv[n, block, :] = convolved
            slope[n, block, :] = GAIN * (0.6 + 0.4 * gate + 0.4 * hidden * (1.0 - gate * gate))

    def arrive(n, index, piece):
        cut = cut_at(segments - 1 - index)
        start, size = rows_of(cut + 1, piece)
        block = slice(start, start + size)
        if index < segments - 1:
            backward_copy(n, piece, cut + 1, index + 1).wait_recv()
        spread(
            spread_g.at[n], gin[n, block, :].astype(F32) * (slope[n, block, :] * demod[n]), start
        )

    def push_back(n, index, piece):
        cut = cut_at(segments - 1 - index)
        start, size = rows_of(cut, piece)
        out = slice(start, start + size)
        back = conv3(spread_g.at[n], flipped, start, size)
        if index > 0:
            gout[n, out, :] = (back * styles[n]).astype(BF16)
            backward_copy(n, piece, cut, index - 1).start()
        d_scaled[n, out, :] = back

    def backward(n, index):
        for piece in range(2):
            arrive(n, index, piece)
            push_back(n, index, piece)

    def channel_sums(n):
        d_hidden = gin[n].astype(F32) * slope[n]
        d_bias[...] += jnp.sum(d_hidden, axis=0, keepdims=True)
        d_demod[n] = jnp.sum(d_hidden * conv[n], axis=0, keepdims=True)
        d_style[n] = jnp.sum(d_scaled[n] * fin[n].astype(F32), axis=0, keepdims=True)

    def add_weight_grad(n):
        for dy in range(3):
            block = jnp.dot(
                turned_x[n], spread_g[n, dy * width:dy * width + pixels, :],
                preferred_element_type=F32,
            )
            for dx in range(3):
                start = ((2 - dy) * 3 + 2 - dx) * chans
                acc[start:start + chans, :] += block[:, dx * chans:(dx + 1) * chans]

    def section(index):
        if index == 0:
            load_images.wait()
        if index > 0:
            flip()
        if index == segments - 1:
            load_cotangent.wait()

        def turn(n, carry):
            turned_x[n] = spread_x[n, middle, chans:2 * chans].T
            return carry

        def forward_step(n, carry):
            forward(n, index)
            if index == segments - 1:
                backward(n, index)
            elif index > 0:
                turn(n, 0)
            return carry

        lax.fori_loop(0, count, forward_step, 0)
        if index == 0:
            flip()
        for k in range(1, replicas):
            latent_copy(k, me).start()
        acc[...] = jnp.zeros_like(acc)

        if index in (0, segments - 1):
            lax.fori_loop(0, count, turn, 0)

        def backward_step(n, carry):
            if index < segments - 1:
                backward(n, index)
            channel_sums(n)
            add_weight_grad(n)
            return carry

        lax.fori_loop(0, count - 1 if index == 0 else count, backward_step, 0)
        if index == 0:
            for piece in range(2):
                arrive(count - 1, index, piece)
            add_weight_grad(count - 1)

        def finish(n, carry):
            for piece in range(2):
                if index < segments - 1:
                    forward_copy(n, piece, cut_at(index), index + 1).wait_send()
                if index > 0:
                    backward_copy(
                        n, piece, cut_at(segments - 1 - index), index - 1
                    ).wait_send()
            return carry

        lax.fori_loop(0, count, finish, 0)

    for index in range(segments):
        pl.when(seg == index)(functools.partial(section, index))

    def acc_share(half, q):
        start = pl.multiple_of((half * chips + q) * share, share)
        return acc[pl.ds(start, share), :]

    def pair_copy(k):
        return remote(pair_out.at[k], pair_in.at[k], a_send.at[k], a_recv.at[k], dp=partner)

    def chip_copy(k):
        return remote(
            chip_out.at[k], chip_in.at[k], b_send.at[k], b_recv.at[k],
            dp=2 * lax.rem(chip + k, chips) + core,
        )

    def shard_copy(k, q):
        return remote(
            wgrad.at[core, q], wgrad.at[core, q], c_send.at[k], c_recv.at[k],
            dp=2 * lax.rem(chip + k, chips) + core,
        )

    def relay_copy(k, half, q):
        return remote(
            wgrad.at[half, q], wgrad.at[half, q], d_send.at[k], d_recv.at[k], dp=partner
        )

    order = list(range(1, chips)) + [0]
    for k in order:
        pair_out[k] = acc_share(1 - core, lax.rem(chip + k, chips)).astype(BF16)
        pair_copy(k).start()

    for k in order:
        pair_copy(k).wait_recv()
        both = acc_share(core, lax.rem(chip + k, chips)) + pair_in[k].astype(F32)
        if k:
            chip_out[k] = both.astype(BF16)
            chip_copy(k).start()
        else:
            own[...] = both

    @pl.when(first)
    def _():
        for piece in range(2):
            push_back(count - 1, 0, piece)
        channel_sums(count - 1)

    style_rows = jnp.concatenate([styles[n] for n in range(count)], axis=0)
    demod_rows = jnp.concatenate([demod[n] for n in range(count)], axis=0)
    d_under = jnp.concatenate([d_demod[n] for n in range(count)], axis=0) * (
        -0.5 * demod_rows * demod_rows * demod_rows
    )
    d_rows = jnp.concatenate([d_style[n] for n in range(count)], axis=0)
    d_rows = d_rows + 2.0 * style_rows * exact(d_under, energy[...], NT)
    rows[me, 0] = d_rows
    rows[me, 1] = d_under
    rows[me, 2] = style_rows * style_rows
    rows[me, 3] = jnp.broadcast_to(d_bias[...], (count, chans))
    for k in range(1, replicas):
        rows_copy(k, me).start()
    parts[seg] = exact(d_rows, affine[...], NT)
    for k in range(1, segments):
        parts_copy(k, seg).start()

    reduced = own[...]
    for k in range(1, chips):
        chip_copy(k).wait_recv()
        reduced += chip_in[k].astype(F32)
    wgrad[core, chip] = reduced.astype(BF16)
    for k in range(1, chips):
        shard_copy(k, chip).start()
    relay_copy(0, core, chip).start()

    for k in range(1, replicas):
        owner = lax.rem(me + replicas - k, replicas)
        latent_copy(k, owner).wait_recv()
        rows_copy(k, owner).wait_recv()
    d_rows = jnp.concatenate([rows[d, 0] for d in range(replicas)], axis=0)
    d_under = jnp.concatenate([rows[d, 1] for d in range(replicas)], axis=0)
    squares = jnp.concatenate([rows[d, 2] for d in range(replicas)], axis=0)
    every = jnp.concatenate([latents[d] for d in range(replicas)], axis=0)
    energy_grad[...] = 2.0 * exact(squares, d_under, TN)
    affine_grad[...] = exact(every, d_rows, TN)
    bias_total = rows[0, 3]
    for d in range(1, replicas):
        bias_total += rows[d, 3]
    bias_grad[...] = bias_total[0:1, :]

    for k in range(1, chips):
        q = lax.rem(chip + chips - k, chips)
        shard_copy(k, q).wait_recv()
        relay_copy(k, core, q).start()

    for k in range(1, segments):
        parts_copy(k, lax.rem(seg + segments - k, segments)).wait_recv()
    latent_total = parts[0]
    for s in range(1, segments):
        latent_total += parts[s]
    latent_grad[...] = latent_total

    for k in range(chips):
        relay_copy(k, 1 - core, lax.rem(chip + chips - k, chips)).wait_recv()

    for k in range(1, replicas):
        latent_copy(k, me).wait_send()
        rows_copy(k, me).wait_send()
    for k in range(1, segments):
        parts_copy(k, seg).wait_send()
    for k in range(chips):
        pair_copy(k).wait_send()
        relay_copy(k, core, lax.rem(chip + chips - k, chips)).wait_send()
        if k:
            chip_copy(k).wait_send()
            shard_copy(k, chip).wait_send()


def results(
    wgrad, weight, energy_grad, affine_in, bias_in, latent_in, weight_out, affine_out, bias_out,
    latent_out, wgrad_here, weight_here, energy_here, out_here, affine_here, bias_here, latent_here,
    in_sems, out_sems, small_sems,
):
    chans = weight.shape[1]
    blocks = [pl.ds(start, chans) for start in range(0, weight.shape[0], chans)]
    loads, stores = [], []
    load_energy = pltpu.make_async_copy(energy_grad, energy_here, small_sems.at[0])
    load_energy.start()
    for tap, block in enumerate(blocks):
        pair = (
            pltpu.make_async_copy(wgrad.at[block], wgrad_here.at[block], in_sems.at[0, tap]),
            pltpu.make_async_copy(weight.at[block], weight_here.at[block], in_sems.at[1, tap]),
        )
        for copy in pair:
            copy.start()
        loads.append(pair)
    small = (
        (affine_in, affine_here, affine_out), (bias_in, bias_here, bias_out),
        (latent_in, latent_here, latent_out),
    )
    for place, (source, held, _) in enumerate(small):
        pltpu.make_async_copy(source, held, small_sems.at[place + 1]).start()
    load_energy.wait()
    for tap, block in enumerate(blocks):
        for copy in loads[tap]:
            copy.wait()
        out_here[block, :] = (
            wgrad_here[block, :].astype(F32)
            + weight_here[block, :].astype(F32) * energy_here[...]
        )
        store = pltpu.make_async_copy(out_here.at[block], weight_out.at[block], out_sems.at[tap])
        store.start()
        stores.append(store)
    for place, (source, held, target) in enumerate(small):
        pltpu.make_async_copy(source, held, small_sems.at[place + 1]).wait()
        store = pltpu.make_async_copy(held, target, out_sems.at[len(blocks) + place])
        store.start()
        stores.append(store)
    for copy in stores:
        copy.wait()


def body(images, latent, weight, affine, biases, cotangent):
    count, height, width, chans = images.shape
    pixels = height * width
    kernel = weight[0]
    segments, replicas = lax.axis_size("segment"), lax.axis_size("dp")
    chips = replicas // 2
    taps = 9 * chans
    share = taps // replicas
    maps = (count, pixels, chans)
    row = (count, 1, chans)
    tall = (count, pixels + 2 * width, 3 * chans)
    vmem = pl.BlockSpec(memory_space=pltpu.VMEM)
    here = pl.BlockSpec(memory_space=pl.ANY)
    dma = pltpu.SemaphoreType.DMA
    wgrad, energy_grad, affine_grad, bias_grad, latent_grad = pl.pallas_call(
        functools.partial(relay, segments, replicas, width),
        out_shape=(
            jax.ShapeDtypeStruct((2, chips, share, chans), BF16),
            jax.ShapeDtypeStruct((chans, chans), F32),
            jax.ShapeDtypeStruct(affine.shape[1:], F32),
            jax.ShapeDtypeStruct((1, chans), F32),
            jax.ShapeDtypeStruct(latent.shape, F32),
        ),
        in_specs=[here] * 6,
        out_specs=(vmem,) * 5,
        scratch_shapes=[
            pltpu.VMEM(maps, BF16), pltpu.VMEM(maps, BF16),
            pltpu.VMEM(maps, BF16), pltpu.VMEM(maps, BF16),
            pltpu.VMEM((3, 3 * chans, chans), BF16),
            pltpu.VMEM(affine.shape[1:], F32),
            pltpu.VMEM((1, chans), F32),
            pltpu.VMEM((replicas,) + latent.shape, F32),
            pltpu.VMEM(tall, BF16),
            pltpu.VMEM((count, chans, pixels), BF16),
            pltpu.VMEM(maps, F32), pltpu.VMEM(maps, F32), pltpu.VMEM(maps, F32),
            pltpu.VMEM((3, 3 * chans, chans), BF16),
            pltpu.VMEM(tall, BF16),
            pltpu.VMEM((taps, chans), F32),
            pltpu.VMEM((chans, chans), F32),
            pltpu.VMEM(row, F32), pltpu.VMEM(row, F32), pltpu.VMEM(row, F32),
            pltpu.VMEM(row, F32), pltpu.VMEM((1, chans), F32),
            pltpu.VMEM((replicas, 4, count, chans), F32),
            pltpu.VMEM((segments,) + latent.shape, F32),
            pltpu.VMEM((chips, share, chans), BF16), pltpu.VMEM((chips, share, chans), BF16),
            pltpu.VMEM((chips, share, chans), BF16), pltpu.VMEM((chips, share, chans), BF16),
            pltpu.VMEM((share, chans), F32),
            dma((count, 2)), dma((count, 2)), dma((count, 2)), dma((count, 2)), dma((6,)),
            dma((replicas,)), dma((replicas,)), dma((replicas,)), dma((replicas,)),
            dma((segments,)), dma((segments,)),
            dma((chips,)), dma((chips,)), dma((chips,)), dma((chips,)),
            dma((chips,)), dma((chips,)), dma((chips,)), dma((chips,)),
        ],
        compiler_params=pltpu.CompilerParams(
            collective_id=0, has_side_effects=True, vmem_limit_bytes=56 * 1024 * 1024
        ),
    )(
        images.reshape(maps), latent, kernel.reshape(3, 3 * chans, chans), affine[0], biases,
        cotangent.reshape(maps),
    )
    small = (affine_grad, bias_grad, latent_grad)
    weight_grad, affine_grad, bias_grad, latent_grad = pl.pallas_call(
        results,
        out_shape=(
            jax.ShapeDtypeStruct((taps, chans), F32),
            *[jax.ShapeDtypeStruct(array.shape, F32) for array in small],
        ),
        in_specs=[here] * 6,
        out_specs=(here,) * 4,
        scratch_shapes=[
            pltpu.VMEM((taps, chans), BF16), pltpu.VMEM((taps, chans), BF16),
            pltpu.VMEM((chans, chans), F32), pltpu.VMEM((taps, chans), F32),
            *[pltpu.VMEM(array.shape, F32) for array in small],
            dma((2, 9)), dma((12,)), dma((4,)),
        ],
        compiler_params=pltpu.CompilerParams(vmem_limit_bytes=56 * 1024 * 1024),
    )(wgrad.reshape(taps, chans), kernel.reshape(taps, chans), energy_grad, *small)
    return (weight_grad.reshape(weight.shape), affine_grad[None], bias_grad, latent_grad)


def solution(mesh):
    placed = (
        P("dp", None, None, None),
        P("dp", None),
        P("segment", None, None, None, None),
        P("segment", None, None),
        P("segment", None),
        P("dp", None, None, None),
    )
    return jax.shard_map(
        body,
        mesh=mesh,
        in_specs=placed,
        out_specs=(
            P("segment", None, None, None, None),
            P("segment", None, None),
            P("segment", None),
            P("dp", None),
        ),
        check_vma=False,
    )
```

```python
import functools
import math

import jax
import jax.numpy as jnp
from jax import lax
from jax.experimental import pallas as pl
from jax.experimental.pallas import tpu as pltpu
from jax.sharding import PartitionSpec as P

GAIN = math.sqrt(2.0)
MESH = pl.DeviceIdType.MESH
F32 = jnp.float32
BF16 = jnp.bfloat16
NN = (((1,), (0,)), ((), ()))
NT = (((1,), (1,)), ((), ()))
TN = (((0,), (0,)), ((), ()))


def exact(a, b, dims):
    return lax.dot_general(
        a, b, dims, precision=lax.Precision.HIGHEST, preferred_element_type=F32
    )


def relay(
    segments, replicas, width,
    images, latent, weight_in, affine_in, biases_in, cotangent,
    wgrad, energy_grad, affine_grad, bias_grad, latent_grad,
    fin, fout, gin, gout, weight, affine, biases, latents,
    spread_x, turned_x, conv, slope, d_scaled, flipped, spread_g, acc, energy,
    styles, demod, d_demod, d_style, d_bias, rows, parts,
    pair_out, pair_in, chip_out, chip_in, own,
    f_send, f_recv, g_send, g_recv, loads, l_send, l_recv, r_send, r_recv, p_send, p_recv,
    a_send, a_recv, b_send, b_recv, c_send, c_recv, d_send, d_recv,
):
    count, pixels, chans = fin.shape
    chips = replicas // 2
    share = acc.shape[0] // replicas
    seg, me = lax.axis_index("segment"), lax.axis_index("dp")
    chip, core = me // 2, lax.rem(me, 2)
    partner = me + 1 - 2 * core
    first, last = seg == 0, seg == segments - 1

    def remote(src, dst, send, recv, **device):
        return pltpu.make_async_remote_copy(
            src_ref=src, dst_ref=dst, send_sem=send, recv_sem=recv,
            device_id=device, device_id_type=MESH,
        )

    load_weight = pltpu.make_async_copy(weight_in, weight, loads.at[0])
    load_affine = pltpu.make_async_copy(affine_in, affine, loads.at[1])
    load_latent = pltpu.make_async_copy(latent, latents.at[me], loads.at[2])
    load_biases = pltpu.make_async_copy(biases_in, biases, loads.at[3])
    load_images = pltpu.make_async_copy(images, fin, loads.at[4])
    load_cotangent = pltpu.make_async_copy(cotangent, gin, loads.at[5])
    load_weight.start()
    load_affine.start()
    load_latent.start()
    load_biases.start()

    @pl.when(first)
    def _():
        load_images.start()

    @pl.when(last)
    def _():
        load_cotangent.start()

    barrier = pltpu.get_barrier_semaphore()
    for k in range(1, replicas):
        pl.semaphore_signal(
            barrier, inc=1, device_id={"dp": lax.rem(me + k, replicas)}, device_id_type=MESH
        )
    for k in range(1, segments):
        pl.semaphore_signal(
            barrier, inc=1, device_id={"segment": lax.rem(seg + k, segments)}, device_id_type=MESH
        )

    def rows_of(cut, piece):
        return (0, cut * width) if piece == 0 else (cut * width, pixels - cut * width)

    def cut_at(hops):
        return pixels // width // 2 + segments // 2 - 1 - hops

    def forward_copy(n, piece, cut, to):
        block = pl.ds(*rows_of(cut, piece))
        return remote(
            fout.at[n, block], fin.at[n, block], f_send.at[n, piece], f_recv.at[n, piece],
            segment=to,
        )

    def backward_copy(n, piece, cut, to):
        block = pl.ds(*rows_of(cut, piece))
        return remote(
            gout.at[n, block], gin.at[n, block], g_send.at[n, piece], g_recv.at[n, piece],
            segment=to,
        )

    def latent_copy(k, owner):
        return remote(
            latents.at[owner], latents.at[owner], l_send.at[k], l_recv.at[k],
            dp=lax.rem(me + k, replicas),
        )

    def rows_copy(k, owner):
        return remote(
            rows.at[owner], rows.at[owner], r_send.at[k], r_recv.at[k],
            dp=lax.rem(me + k, replicas),
        )

    def parts_copy(k, owner):
        return remote(
            parts.at[owner], parts.at[owner], p_send.at[k], p_recv.at[k],
            segment=lax.rem(seg + k, segments),
        )

    middle = slice(width, width + pixels)

    def spread(target, value, start):
        size = value.shape[0]
        column = lax.rem(lax.broadcasted_iota(jnp.int32, (size, chans), 0), width)
        block = slice(width + start, width + start + size)
        target[block, chans:2 * chans] = value.astype(BF16)
        target[block, :chans] = jnp.where(
            column == 0, 0.0, pltpu.roll(value, 1, 0)
        ).astype(BF16)
        target[block, 2 * chans:] = jnp.where(
            column == width - 1, 0.0, pltpu.roll(value, size - 1, 0)
        ).astype(BF16)

    def conv3(source, kernel, start, size):
        total = jnp.dot(source[start:start + size, :], kernel[0], preferred_element_type=F32)
        for dy in (1, 2):
            at = start + dy * width
            total += jnp.dot(source[at:at + size, :], kernel[dy], preferred_element_type=F32)
        return total

    edge = jnp.zeros((width, 3 * chans), BF16)
    for n in range(count):
        for target in (spread_x, spread_g):
            target[n, 0:width, :] = edge
            target[n, width + pixels:, :] = edge
    d_bias[...] = jnp.zeros_like(d_bias)
    load_weight.wait()
    total = jnp.zeros((chans, chans), F32)
    for dy in range(3):
        for dx in range(3):
            total += jnp.square(weight[dy, dx * chans:(dx + 1) * chans, :].astype(F32))
    energy[...] = total
    load_affine.wait()
    load_latent.wait()
    load_biases.wait()
    style_rows = exact(latents[me], affine[...], NN) + 1.0
    demod_rows = lax.rsqrt(exact(style_rows * style_rows, total, NN) + 1e-08)
    for n in range(count):
        styles[n] = style_rows[n:n + 1, :]
        demod[n] = demod_rows[n:n + 1, :]

    def flip():
        for dy in range(3):
            for dx in range(3):
                part = weight[2 - dy, (2 - dx) * chans:(3 - dx) * chans, :]
                flipped[dy, dx * chans:(dx + 1) * chans, :] = part.T

    pl.semaphore_wait(barrier, replicas + segments - 2)

    def slope_of(hidden, gate):
        return GAIN * (0.6 + 0.4 * gate + 0.4 * hidden * (1.0 - gate * gate))

    def forward(n, index):
        cut = cut_at(index)
        for piece in range(2):
            start, size = rows_of(cut + 1, piece)
            if index > 0:
                forward_copy(n, piece, cut + 1, index - 1).wait_recv()
            spread(
                spread_x.at[n], fin[n, start:start + size, :].astype(F32) * styles[n], start
            )
            start, size = rows_of(cut, piece)
            block = slice(start, start + size)
            convolved = conv3(spread_x.at[n], weight, start, size)
            hidden = convolved * demod[n] + biases[...]
            gate = jnp.tanh(hidden)
            if index < segments - 1:
                fout[n, block, :] = (GAIN * hidden * (0.6 + 0.4 * gate)).astype(BF16)
                forward_copy(n, piece, cut, index + 1).start()
            conv[n, block, :] = convolved
            if index > 0:
                slope[n, block, :] = slope_of(hidden, gate)

    def arrive(n, index, piece):
        cut = cut_at(segments - 1 - index)
        start, size = rows_of(cut + 1, piece)
        block = slice(start, start + size)
        if index < segments - 1:
            backward_copy(n, piece, cut + 1, index + 1).wait_recv()
        spread(
            spread_g.at[n], gin[n, block, :].astype(F32) * (slope[n, block, :] * demod[n]), start
        )

    def push_back(n, index, piece):
        cut = cut_at(segments - 1 - index)
        start, size = rows_of(cut, piece)
        out = slice(start, start + size)
        back = conv3(spread_g.at[n], flipped, start, size)
        if index > 0:
            gout[n, out, :] = (back * styles[n]).astype(BF16)
            backward_copy(n, piece, cut, index - 1).start()
        d_scaled[n, out, :] = back

    def backward(n, index):
        for piece in range(2):
            arrive(n, index, piece)
            push_back(n, index, piece)

    def channel_sums(n):
        d_hidden = gin[n].astype(F32) * slope[n]
        d_bias[...] += jnp.sum(d_hidden, axis=0, keepdims=True)
        d_demod[n] = jnp.sum(d_hidden * conv[n], axis=0, keepdims=True)
        d_style[n] = jnp.sum(d_scaled[n] * fin[n].astype(F32), axis=0, keepdims=True)

    def add_weight_grad(n):
        for dy in range(3):
            block = jnp.dot(
                turned_x[n], spread_g[n, dy * width:dy * width + pixels, :],
                preferred_element_type=F32,
            )
            for dx in range(3):
                start = ((2 - dy) * 3 + 2 - dx) * chans
                acc[start:start + chans, :] += block[:, dx * chans:(dx + 1) * chans]

    def section(index):
        if index == 0:
            load_images.wait()
        if index > 0:
            flip()
        if index == segments - 1:
            load_cotangent.wait()

        def turn(n, carry):
            turned_x[n] = spread_x[n, middle, chans:2 * chans].T
            return carry

        def forward_step(n, carry):
            forward(n, index)
            if index == segments - 1:
                backward(n, index)
            elif index > 0:
                turn(n, 0)
            return carry

        lax.fori_loop(0, count, forward_step, 0)
        if index == 0:
            flip()

            def steepen(n, carry):
                hidden = conv[n] * demod[n] + biases[...]
                slope[n] = slope_of(hidden, jnp.tanh(hidden))
                return carry

            lax.fori_loop(0, count, steepen, 0)
        for k in range(1, replicas):
            latent_copy(k, me).start()
        acc[...] = jnp.zeros_like(acc)

        if index in (0, segments - 1):
            lax.fori_loop(0, count, turn, 0)

        def backward_step(n, carry):
            if index < segments - 1:
                backward(n, index)
            channel_sums(n)
            add_weight_grad(n)
            return carry

        lax.fori_loop(0, count - 1 if index == 0 else count, backward_step, 0)
        if index == 0:
            for piece in range(2):
                arrive(count - 1, index, piece)
            add_weight_grad(count - 1)

        def finish(n, carry):
            for piece in range(2):
                if index < segments - 1:
                    forward_copy(n, piece, cut_at(index), index + 1).wait_send()
                if index > 0:
                    backward_copy(
                        n, piece, cut_at(segments - 1 - index), index - 1
                    ).wait_send()
            return carry

        lax.fori_loop(0, count, finish, 0)

    for index in range(segments):
        pl.when(seg == index)(functools.partial(section, index))

    def acc_share(half, q):
        start = pl.multiple_of((half * chips + q) * share, share)
        return acc[pl.ds(start, share), :]

    def pair_copy(k):
        return remote(pair_out.at[k], pair_in.at[k], a_send.at[k], a_recv.at[k], dp=partner)

    def chip_copy(k):
        return remote(
            chip_out.at[k], chip_in.at[k], b_send.at[k], b_recv.at[k],
            dp=2 * lax.rem(chip + k, chips) + core,
        )

    def shard_copy(k, q):
        return remote(
            wgrad.at[core, q], wgrad.at[core, q], c_send.at[k], c_recv.at[k],
            dp=2 * lax.rem(chip + k, chips) + core,
        )

    def relay_copy(k, half, q):
        return remote(
            wgrad.at[half, q], wgrad.at[half, q], d_send.at[k], d_recv.at[k], dp=partner
        )

    order = list(range(1, chips)) + [0]
    for k in order:
        pair_out[k] = acc_share(1 - core, lax.rem(chip + k, chips)).astype(BF16)
        pair_copy(k).start()

    for k in order:
        pair_copy(k).wait_recv()
        both = acc_share(core, lax.rem(chip + k, chips)) + pair_in[k].astype(F32)
        if k:
            chip_out[k] = both.astype(BF16)
            chip_copy(k).start()
        else:
            own[...] = both

    @pl.when(first)
    def _():
        for piece in range(2):
            push_back(count - 1, 0, piece)
        channel_sums(count - 1)

    style_rows = jnp.concatenate([styles[n] for n in range(count)], axis=0)
    demod_rows = jnp.concatenate([demod[n] for n in range(count)], axis=0)
    d_under = jnp.concatenate([d_demod[n] for n in range(count)], axis=0) * (
        -0.5 * demod_rows * demod_rows * demod_rows
    )
    d_rows = jnp.concatenate([d_style[n] for n in range(count)], axis=0)
    d_rows = d_rows + 2.0 * style_rows * exact(d_under, energy[...], NT)
    rows[me, 0] = d_rows
    rows[me, 1] = d_under
    rows[me, 2] = style_rows * style_rows
    rows[me, 3] = jnp.broadcast_to(d_bias[...], (count, chans))
    for k in range(1, replicas):
        rows_copy(k, me).start()
    parts[seg] = exact(d_rows, affine[...], NT)
    for k in range(1, segments):
        parts_copy(k, seg).start()

    reduced = own[...]
    for k in range(1, chips):
        chip_copy(k).wait_recv()
        reduced += chip_in[k].astype(F32)
    wgrad[core, chip] = reduced.astype(BF16)
    for k in range(1, chips):
        shard_copy(k, chip).start()
    relay_copy(0, core, chip).start()

    for k in range(1, replicas):
        owner = lax.rem(me + replicas - k, replicas)
        latent_copy(k, owner).wait_recv()
        rows_copy(k, owner).wait_recv()
    d_rows = jnp.concatenate([rows[d, 0] for d in range(replicas)], axis=0)
    d_under = jnp.concatenate([rows[d, 1] for d in range(replicas)], axis=0)
    squares = jnp.concatenate([rows[d, 2] for d in range(replicas)], axis=0)
    every = jnp.concatenate([latents[d] for d in range(replicas)], axis=0)
    energy_grad[...] = 2.0 * exact(squares, d_under, TN)
    affine_grad[...] = exact(every, d_rows, TN)
    bias_total = rows[0, 3]
    for d in range(1, replicas):
        bias_total += rows[d, 3]
    bias_grad[...] = bias_total[0:1, :]

    for k in range(1, chips):
        q = lax.rem(chip + chips - k, chips)
        shard_copy(k, q).wait_recv()
        relay_copy(k, core, q).start()

    for k in range(1, segments):
        parts_copy(k, lax.rem(seg + segments - k, segments)).wait_recv()
    latent_total = parts[0]
    for s in range(1, segments):
        latent_total += parts[s]
    latent_grad[...] = latent_total

    for k in range(chips):
        relay_copy(k, 1 - core, lax.rem(chip + chips - k, chips)).wait_recv()

    for k in range(1, replicas):
        latent_copy(k, me).wait_send()
        rows_copy(k, me).wait_send()
    for k in range(1, segments):
        parts_copy(k, seg).wait_send()
    for k in range(chips):
        pair_copy(k).wait_send()
        relay_copy(k, core, lax.rem(chip + chips - k, chips)).wait_send()
        if k:
            chip_copy(k).wait_send()
            shard_copy(k, chip).wait_send()


def results(
    wgrad, weight, energy_grad, affine_in, bias_in, latent_in, weight_out, affine_out, bias_out,
    latent_out, wgrad_here, weight_here, energy_here, out_here, affine_here, bias_here, latent_here,
    in_sems, out_sems, small_sems,
):
    chans = weight.shape[1]
    blocks = [pl.ds(start, chans) for start in range(0, weight.shape[0], chans)]
    loads, stores = [], []
    load_energy = pltpu.make_async_copy(energy_grad, energy_here, small_sems.at[0])
    load_energy.start()
    for tap, block in enumerate(blocks):
        pair = (
            pltpu.make_async_copy(wgrad.at[block], wgrad_here.at[block], in_sems.at[0, tap]),
            pltpu.make_async_copy(weight.at[block], weight_here.at[block], in_sems.at[1, tap]),
        )
        for copy in pair:
            copy.start()
        loads.append(pair)
    small = (
        (affine_in, affine_here, affine_out), (bias_in, bias_here, bias_out),
        (latent_in, latent_here, latent_out),
    )
    for place, (source, held, _) in enumerate(small):
        pltpu.make_async_copy(source, held, small_sems.at[place + 1]).start()
    load_energy.wait()
    for tap, block in enumerate(blocks):
        for copy in loads[tap]:
            copy.wait()
        out_here[block, :] = (
            wgrad_here[block, :].astype(F32)
            + weight_here[block, :].astype(F32) * energy_here[...]
        )
        store = pltpu.make_async_copy(out_here.at[block], weight_out.at[block], out_sems.at[tap])
        store.start()
        stores.append(store)
    for place, (source, held, target) in enumerate(small):
        pltpu.make_async_copy(source, held, small_sems.at[place + 1]).wait()
        store = pltpu.make_async_copy(held, target, out_sems.at[len(blocks) + place])
        store.start()
        stores.append(store)
    for copy in stores:
        copy.wait()


def body(images, latent, weight, affine, biases, cotangent):
    count, height, width, chans = images.shape
    pixels = height * width
    kernel = weight[0]
    segments, replicas = lax.axis_size("segment"), lax.axis_size("dp")
    chips = replicas // 2
    taps = 9 * chans
    share = taps // replicas
    maps = (count, pixels, chans)
    row = (count, 1, chans)
    tall = (count, pixels + 2 * width, 3 * chans)
    vmem = pl.BlockSpec(memory_space=pltpu.VMEM)
    here = pl.BlockSpec(memory_space=pl.ANY)
    dma = pltpu.SemaphoreType.DMA
    wgrad, energy_grad, affine_grad, bias_grad, latent_grad = pl.pallas_call(
        functools.partial(relay, segments, replicas, width),
        out_shape=(
            jax.ShapeDtypeStruct((2, chips, share, chans), BF16),
            jax.ShapeDtypeStruct((chans, chans), F32),
            jax.ShapeDtypeStruct(affine.shape[1:], F32),
            jax.ShapeDtypeStruct((1, chans), F32),
            jax.ShapeDtypeStruct(latent.shape, F32),
        ),
        in_specs=[here] * 6,
        out_specs=(vmem,) * 5,
        scratch_shapes=[
            pltpu.VMEM(maps, BF16), pltpu.VMEM(maps, BF16),
            pltpu.VMEM(maps, BF16), pltpu.VMEM(maps, BF16),
            pltpu.VMEM((3, 3 * chans, chans), BF16),
            pltpu.VMEM(affine.shape[1:], F32),
            pltpu.VMEM((1, chans), F32),
            pltpu.VMEM((replicas,) + latent.shape, F32),
            pltpu.VMEM(tall, BF16),
            pltpu.VMEM((count, chans, pixels), BF16),
            pltpu.VMEM(maps, F32), pltpu.VMEM(maps, F32), pltpu.VMEM(maps, F32),
            pltpu.VMEM((3, 3 * chans, chans), BF16),
            pltpu.VMEM(tall, BF16),
            pltpu.VMEM((taps, chans), F32),
            pltpu.VMEM((chans, chans), F32),
            pltpu.VMEM(row, F32), pltpu.VMEM(row, F32), pltpu.VMEM(row, F32),
            pltpu.VMEM(row, F32), pltpu.VMEM((1, chans), F32),
            pltpu.VMEM((replicas, 4, count, chans), F32),
            pltpu.VMEM((segments,) + latent.shape, F32),
            pltpu.VMEM((chips, share, chans), BF16), pltpu.VMEM((chips, share, chans), BF16),
            pltpu.VMEM((chips, share, chans), BF16), pltpu.VMEM((chips, share, chans), BF16),
            pltpu.VMEM((share, chans), F32),
            dma((count, 2)), dma((count, 2)), dma((count, 2)), dma((count, 2)), dma((6,)),
            dma((replicas,)), dma((replicas,)), dma((replicas,)), dma((replicas,)),
            dma((segments,)), dma((segments,)),
            dma((chips,)), dma((chips,)), dma((chips,)), dma((chips,)),
            dma((chips,)), dma((chips,)), dma((chips,)), dma((chips,)),
        ],
        compiler_params=pltpu.CompilerParams(
            collective_id=0, has_side_effects=True, vmem_limit_bytes=56 * 1024 * 1024
        ),
    )(
        images.reshape(maps), latent, kernel.reshape(3, 3 * chans, chans), affine[0], biases,
        cotangent.reshape(maps),
    )
    small = (affine_grad, bias_grad, latent_grad)
    weight_grad, affine_grad, bias_grad, latent_grad = pl.pallas_call(
        results,
        out_shape=(
            jax.ShapeDtypeStruct((taps, chans), F32),
            *[jax.ShapeDtypeStruct(array.shape, F32) for array in small],
        ),
        in_specs=[here] * 6,
        out_specs=(here,) * 4,
        scratch_shapes=[
            pltpu.VMEM((taps, chans), BF16), pltpu.VMEM((taps, chans), BF16),
            pltpu.VMEM((chans, chans), F32), pltpu.VMEM((taps, chans), F32),
            *[pltpu.VMEM(array.shape, F32) for array in small],
            dma((2, 9)), dma((12,)), dma((4,)),
        ],
        compiler_params=pltpu.CompilerParams(vmem_limit_bytes=56 * 1024 * 1024),
    )(wgrad.reshape(taps, chans), kernel.reshape(taps, chans), energy_grad, *small)
    return (weight_grad.reshape(weight.shape), affine_grad[None], bias_grad, latent_grad)


def solution(mesh):
    placed = (
        P("dp", None, None, None),
        P("dp", None),
        P("segment", None, None, None, None),
        P("segment", None, None),
        P("segment", None),
        P("dp", None, None, None),
    )
    return jax.shard_map(
        body,
        mesh=mesh,
        in_specs=placed,
        out_specs=(
            P("segment", None, None, None, None),
            P("segment", None, None),
            P("segment", None),
            P("dp", None),
        ),
        check_vma=False,
    )
```
